1024 devices in a mesh: dp: 16 (over z_lo), ctx: 4 (over x), ep: 16 (over z_hi, y, core).
Axes of the slice: x: 4, y: 4, z: 32 (z_hi: 2, z_lo: 16; z = z_hi * 16 + z_lo), core: 2. Of those that a mesh axis runs over, the one named last changes fastest.
Arguments:
- tokens: bfloat16 [32768, 4096], P(('dp', 'ep'), 'ctx'), may hold values from -24 to 24
- routes: int32 [32768, 1], P(('dp', 'ep')), may hold values from 0 to 15; in each aligned block of 128 rows (0 to 127, 128 to 255, ...) at most 10 rows name the same one
- router_weight: float32 [4096, 16], replicated, may hold values from -0.09375 to 0.09375
- gate_weight: bfloat16 [16, 4096, 1024], P('ep', 'ctx'), may hold values from -0.09375 to 0.09375
- up_weight: bfloat16 [16, 4096, 1024], P('ep', 'ctx'), may hold values from -0.09375 to 0.09375
- down_weight: bfloat16 [16, 1024, 4096], P('ep', None, 'ctx'), may hold values from -0.1875 to 0.1875
- cotangent: bfloat16 [32768, 4096], P(('dp', 'ep'), 'ctx'), may hold values from -0.03125 to 0.03125
Outputs:
- block_out: bfloat16 [32768, 4096], P(('dp', 'ep'), 'ctx')
- router_grad: float32 [4096, 16], P('ctx')
The draws below stay inside these ranges and needn't reach their ends.
Inputs may be any that keep to these rules, and one draw needn't show every extreme that they name: `routes`: within each aligned block of 128 rows no expert is named by more than 10 rows, a bound that some block reaches.
All inputs are finite; a program needn't handle non-finite values.
Results may differ from the reference program's by a relative error of at most 0.023.
Values may be sent and summed in bfloat16 or wider, within the bound.
No kernel may reach another device: no remote copies, remote signals or barrier semaphores. Data moves between devices by JAX's collectives and lax.ppermute only.
A program may use at most 32 MiB of HBM per device.

```python
import math
import jax
import jax.numpy as jnp
import numpy as np
from jax import lax

D = 4096
HIDDEN_SIZE = 1024
TOK_DEV = 128
EXPERTS = 16
CAP = 10
TOKENS = 32768
N_DP = 16
N_CTX = 4
N_EP = 16


def with_spikes(drawn, rng, source, target, shards_of, factor):
    owner, partner = [(jnp.arange(drawn.shape[dim]) // (drawn.shape[dim] // shards_of)).reshape([-1 if axis == dim else 1 for axis in range(drawn.ndim)]) for dim in (source, target)]
    chosen = jax.random.permutation(rng, shards_of)[partner]
    strong = (owner == chosen) | (owner == (partner + shards_of // 2) % shards_of)
    return jnp.where(strong, factor * drawn, drawn)


def level_of(own_key, extent, split, least, high):
    factor_of, own = 1.0, jax.random.fold_in(own_key, 6)
    for position, blocks in split:
        draws = jnp.exp(jax.random.uniform(jax.random.fold_in(own, position), (blocks,), jnp.float32, least / len(split), high / len(split)))
        factor_of = factor_of * jnp.repeat(draws, extent[position] // blocks).reshape([-1 if axis == position else 1 for axis in range(len(extent))])
    return factor_of


def assign_block(key, own, number, rows, count, top, reach, skew):
    ranking = jax.random.permutation(key, count)
    crowded, usual = load_shares(count, rows * top, reach, skew, True), load_shares(count, rows * top, reach, skew, False)
    places = jnp.arange(count)

    def named(lengths, turn):
        used = int((lengths > 0).sum())
        fixed = max(1, used // 4)
        passed = fixed + (places - fixed + turn * (used - fixed)) % max(1, count - fixed)
        return jnp.zeros((count,), jnp.int32).at[ranking[jnp.where(places < fixed, places, passed)]].set(jnp.asarray(lengths, jnp.int32))

    lengths = jnp.where(number % 4 == 0, named(crowded, number // 4), named(usual, number - number // 4 - 1))
    mixed = jax.random.permutation(jax.random.fold_in(own, 3), count)
    source_of, receiver = mixed[0:count // 2 * 2:2], mixed[1:count // 2 * 2:2]
    margin = jnp.minimum(lengths[source_of] - 1, reach - lengths[receiver]) // 2
    margin = jnp.where((source_of == ranking[0]) | (receiver == ranking[0]) | (lengths[receiver] == 0), 0, jnp.maximum(margin, 0))
    passed = jax.random.randint(jax.random.fold_in(own, 4), (count // 2,), 0, 1 << 20) % (margin + 1)
    lengths = lengths.at[source_of].add(-passed).at[receiver].add(passed)
    items = jnp.searchsorted(jnp.cumsum(lengths), jnp.arange(rows * top), side="right").astype(jnp.int32)
    listing = items.reshape(top, rows).T
    listing = listing[jax.random.permutation(jax.random.fold_in(own, 1), rows)]
    turn = jax.random.randint(jax.random.fold_in(own, 2), (rows, 1), 0, top)
    return jnp.take_along_axis(listing, (jnp.arange(top)[None, :] + turn) % top, axis=1)


def load_shares(amount, total, most, skew, full):
    weights = [(1 << 20) // math.isqrt(rank ** skew) + 1 for rank in range(1, amount + 1)]
    largest = most if full else min(most, max(-(-total // amount), total * weights[0] // sum(weights)))
    least = 1 if total - largest >= amount - 1 else 0
    given, spare = [largest] + [least] * (amount - 1), total - largest - least * (amount - 1)
    while spare > 0:
        candidates = [i for i in range(1, amount) if given[i] < largest] or [i for i in range(1, amount) if given[i] < most]
        pool, budget = sum([weights[i] for i in candidates]), spare
        for i in candidates:
            more = min(most - given[i], max(1, budget * weights[i] // pool), spare)
            given[i] = given[i] + more
            spare = spare - more
    return np.array(given)


def normal_values(stream_key, extent, spread, reach, pieces=(), kind=jnp.bfloat16):
    array = jax.random.normal(stream_key, extent, jnp.float32) * spread
    if len(pieces) > 0:
        array = level_of(stream_key, extent, pieces, -0.22, 0.18) * array
    return jnp.clip(array, min=-reach, max=reach).astype(kind)


def bell_draw_with(stream_key, shape, width, most, shards, heavy, kind=jnp.bfloat16):
    drawn = width * jax.random.normal(stream_key, shape, jnp.float32)
    if shards:
        drawn = drawn * level_of(stream_key, shape, shards, -0.22, 0.18)
    return jnp.clip(with_spikes(drawn, jax.random.fold_in(stream_key, 3), *heavy), -most, most).astype(kind)


def setup_inputs(seed: int = 0) -> dict:
    key_list = jax.random.split(jax.random.key(seed), 8)
    tokens = bell_draw_with(key_list[0], (TOKENS, D), 1.0, 24.0, ((0, 256), (1, 4)), (0, 1, 256, 6.0))
    routes_keys = jax.random.split(jax.random.fold_in(key_list[1], 1), TOKENS // TOK_DEV)
    routes_turns = jax.random.permutation(jax.random.fold_in(key_list[1], 3), TOKENS // TOK_DEV)
    routes = jax.vmap(lambda own, number: assign_block(jax.random.fold_in(key_list[1], 2), own, number, TOK_DEV, EXPERTS, 1, CAP, 2))(routes_keys, routes_turns).reshape((TOKENS, 1))
    router_weight = normal_values(key_list[2], (D, EXPERTS), D ** -0.5, 0.09375, (), jnp.float32)
    gate_weight = normal_values(key_list[3], (EXPERTS, D, HIDDEN_SIZE), D ** -0.5, 0.09375, ((0, 16), (1, 4)))
    up_weight = normal_values(key_list[4], (EXPERTS, D, HIDDEN_SIZE), D ** -0.5, 0.09375, ((0, 16), (1, 4)))
    down_weight = normal_values(key_list[5], (EXPERTS, HIDDEN_SIZE, D), HIDDEN_SIZE ** -0.5, 0.1875, ((0, 16), (2, 4)))
    cotangent = normal_values(key_list[6], (TOKENS, D), (0.1 * (EXPERTS / TOKENS) ** 0.5), 0.03125, ((0, 256), (1, 4)))
    return dict(tokens=tokens, routes=routes, router_weight=router_weight, gate_weight=gate_weight, up_weight=up_weight, down_weight=down_weight, cotangent=cotangent)


def expert_rows(row_block, gate_matrix, up_matrix, down_matrix):
    quarter = row_block.shape[1] // N_CTX
    gate_sum = jnp.zeros((row_block.shape[0], gate_matrix.shape[1]), jnp.float32)
    up_sum = jnp.zeros((row_block.shape[0], up_matrix.shape[1]), jnp.float32)
    for section in range(N_CTX):
        portion = row_block[:, section * quarter:(section + 1) * quarter]
        gate_term = jnp.dot(portion, gate_matrix[section * quarter:(section + 1) * quarter], preferred_element_type=jnp.float32)
        up_term = jnp.dot(portion, up_matrix[section * quarter:(section + 1) * quarter], preferred_element_type=jnp.float32)
        gate_sum = gate_sum + lax.optimization_barrier(gate_term.astype(jnp.bfloat16)).astype(jnp.float32)
        up_sum = up_sum + lax.optimization_barrier(up_term.astype(jnp.bfloat16)).astype(jnp.float32)
    hidden = (jax.nn.silu(gate_sum) * up_sum).astype(jnp.bfloat16)
    return jnp.dot(hidden, down_matrix, preferred_element_type=jnp.float32).astype(jnp.bfloat16)


def reference(tokens, routes, router_weight, gate_weight, up_weight, down_weight, cotangent):
    route = routes[:, 0].astype(jnp.int32)
    order = jnp.argsort(route, stable=True).astype(jnp.int32)
    expert_ids = jnp.arange(EXPERTS, dtype=jnp.int32)
    counts = jnp.sum((route[:, None] == expert_ids[None, :]).astype(jnp.int32), axis=0)
    starts = (jnp.cumsum(counts) - counts).astype(jnp.int32)
    bound = N_DP * N_EP * CAP
    padded = jnp.concatenate([order, jnp.full((bound,), TOKENS, jnp.int32)])
    expert_out = jnp.zeros((TOKENS, D), jnp.bfloat16)
    for expert in range(EXPERTS):
        chosen = lax.dynamic_slice(padded, (starts[expert],), (bound,))
        live = jnp.arange(bound, dtype=jnp.int32) < counts[expert]
        chosen = jnp.where(live, chosen, TOKENS).astype(jnp.int32)
        gathered = jnp.take(tokens, chosen, axis=0, mode="fill", fill_value=0)
        result = expert_rows(gathered, gate_weight[expert], up_weight[expert], down_weight[expert])
        expert_out = expert_out.at[chosen].set(result, mode="drop")

    def token_block(total, blocks):
        tok_block, route_block, out_block, cot_block = blocks
        logits = jnp.dot(tok_block.astype(jnp.float32), router_weight, precision=lax.Precision.HIGHEST)
        onehot = (route_block[:, None] == expert_ids[None, :]).astype(jnp.float32)
        score = jax.nn.sigmoid(jnp.sum(logits * onehot, axis=1))
        values = out_block.astype(jnp.float32)
        mixed = (score[:, None] * values).astype(jnp.bfloat16)
        slope = jnp.sum(cot_block.astype(jnp.float32) * values, axis=1) * score * (1.0 - score)
        coefs = onehot * slope[:, None]
        total = total + jnp.dot(tok_block.astype(jnp.float32).T, coefs, precision=lax.Precision.HIGHEST)
        return total, mixed

    blocks = (tokens.reshape(-1, TOK_DEV, D), route.reshape(-1, TOK_DEV),
              expert_out.reshape(-1, TOK_DEV, D), cotangent.reshape(-1, TOK_DEV, D))
    router_grad, mixed = lax.scan(token_block, jnp.zeros((D, EXPERTS), jnp.float32), blocks)
    return mixed.reshape(TOKENS, D), router_grad
```

```python
import jax
import jax.numpy as jnp
from jax import lax
from jax.sharding import Mesh, PartitionSpec as P

BF16 = jnp.bfloat16
F32 = jnp.float32
N_EP = 16
N_CTX = 4
ROUTE = ("dh", "zh", "y", "core")
ALL_Z = ("dh", "dl", "zh")
IN_Z = ("y", "core")


def route_groups():
    groups = []
    for flip in (0, 1):
        groups.append([(((e >> 3) ^ flip) * 2 + (e >> 3)) * 8 + (e & 7) for e in range(N_EP)])
    return groups


def split(v, parts):
    out = []
    for _ in range(parts):
        p = v.astype(BF16)
        out.append(p)
        v = v - p.astype(F32)
    return jnp.stack(out, axis=-1)


def dot(a, b, dims=((1,), (0,))):
    return lax.dot_general(a, b, (dims, ((), ())), preferred_element_type=F32)


def shards(tokens, routes, router_weight, gate_weight, up_weight, down_weight, cotangent):
    tok_count, width = tokens.shape
    capacity = 5 * tok_count // (4 * N_EP)
    rows = N_EP * capacity
    groups = route_groups()
    expert = lax.axis_index("zh") * 8 + lax.axis_index("y") * 2 + lax.axis_index("core")
    route = routes[:, 0]
    expert_ids = jnp.arange(N_EP, dtype=jnp.int32)
    onehot = (route[:, None] == expert_ids[None, :]).astype(jnp.int32)
    earlier = jnp.cumsum(onehot, axis=0) - onehot
    position = jnp.sum(earlier * onehot, axis=1)
    slot = route * capacity + position
    slot_ids = jnp.arange(rows, dtype=jnp.int32)
    placement = (slot[None, :] == slot_ids[:, None]).astype(BF16)
    both = jnp.concatenate([tokens, cotangent], axis=1)
    outgoing = dot(placement, both).astype(BF16)
    received = lax.all_to_all(outgoing, ROUTE, 0, 0, axis_index_groups=groups, tiled=True)
    x, cot = received[:, :width], received[:, width:]

    router_rows = lax.dynamic_slice_in_dim(router_weight, lax.axis_index("ctx") * width, width, 0)
    router_col = lax.dynamic_slice_in_dim(router_rows, expert, 1, 1)[:, 0]
    gate_part = dot(x, gate_weight[0]).astype(BF16)
    up_part = dot(x, up_weight[0]).astype(BF16)
    back_part = dot(cot, down_weight[0], ((1,), (1,))).astype(BF16)
    logit_part = jnp.sum(dot(x, split(router_col, 3)), axis=1)
    small = jnp.pad(split(logit_part, 3), ((0, 0), (0, 125)))
    parts = jnp.concatenate([gate_part, up_part, back_part, small], axis=1)
    mine = lax.all_to_all(parts, "ctx", 0, 0, tiled=True)
    sums = jnp.sum(mine.reshape(N_CTX, rows // N_CTX, -1).astype(F32), axis=0)
    h = gate_part.shape[1]
    gate, up, back = sums[:, :h], sums[:, h : 2 * h], sums[:, 2 * h : 3 * h]
    logit = jnp.sum(sums[:, 3 * h :], axis=1)
    hidden = (jax.nn.silu(gate) * up).astype(BF16)
    inner = jnp.sum(hidden.astype(F32) * back, axis=1)
    score = jax.nn.sigmoid(logit)
    slope = inner * score * (1.0 - score)
    small = jnp.pad(jnp.concatenate([split(score, 3), split(slope, 3)], axis=1), ((0, 0), (0, 122)))
    full = lax.all_gather(jnp.concatenate([hidden, small], axis=1), "ctx", axis=0, tiled=True)
    values = dot(full[:, :h], down_weight[0]).astype(BF16).astype(F32)
    score = jnp.sum(full[:, h : h + 3].astype(F32), axis=1)
    block_rows = (score[:, None] * values).astype(BF16)
    grad = jnp.sum(dot(full[:, h + 3 : h + 6], x, ((0,), (0,))), axis=0)
    returned = lax.all_to_all(block_rows, ROUTE, 0, 0, axis_index_groups=groups, tiled=True)
    block_out = dot(placement, returned, ((0,), (0,))).astype(BF16)

    grads = lax.all_to_all(jnp.broadcast_to(grad.reshape(1, 8, -1), (32, 8, width // 8)), ALL_Z, 0, 0, tiled=True)
    grads = jnp.sum(grads.reshape(16, 2, 1, 8, -1), axis=0)
    grads = jnp.broadcast_to(grads.reshape(1, 16, -1), (8, 16, width // 8))
    grads = lax.all_to_all(grads, IN_Z, 0, 0, tiled=True)
    router_grad = grads.reshape(8, 2, width).transpose(2, 1, 0).reshape(width, N_EP)
    return (block_out, router_grad)


def solution(mesh):
    fine = Mesh(mesh.devices.reshape(2, 8, 4, 2, 4, 2), ("dh", "dl", "ctx", "zh", "y", "core"))
    tok = ("dh", "dl", "zh", "y", "core")
    ep = ("zh", "y", "core")
    return jax.shard_map(
        shards,
        mesh=fine,
        in_specs=(
            P(tok, "ctx"),
            P(tok, None),
            P(),
            P(ep, "ctx", None),
            P(ep, "ctx", None),
            P(ep, None, "ctx"),
            P(tok, "ctx"),
        ),
        out_specs=(P(tok, "ctx"), P("ctx", None)),
        check_vma=False,
    )
```

```python
import functools

import jax
import jax.numpy as jnp
from jax import lax
from jax.experimental import pallas as pl
from jax.experimental.pallas import tpu as pltpu
from jax.sharding import Mesh, PartitionSpec as P

BF16 = jnp.bfloat16
F32 = jnp.float32
I32 = jnp.int32
CAP = 10
N_EXP = 16
N_CTX = 4
HALF = 8
PART = 16
BACK = 8
MESH = (2, 8, 4, 2, 4, 2)
NAMES = ("dh", "dl", "ctx", "zh", "y", "core")
TOK = ("dh", "dl", "zh", "y", "core")
ALL_Z = ("dh", "dl", "zh")
IN_Z = ("y", "core")
PAIR = ("dh", "zh")
PAIR_PERM = ((0, 3), (3, 0), (1, 2), (2, 1))


def dot(a, b, dims=((1,), (0,))):
    return lax.dot_general(a, b, (dims, ((), ())), preferred_element_type=F32)


def iota(shape, dim):
    return lax.broadcasted_iota(I32, shape, dim)


def pick(mask):
    return mask.astype(F32).astype(BF16)


def pieces(v):
    a = v.astype(BF16)
    v = v - a.astype(F32)
    b = v.astype(BF16)
    c = (v - b.astype(F32)).astype(BF16)
    return a, b, c


def spread(lane, first, v):
    a, b, c = pieces(v)
    out = jnp.where(lane == first, a.astype(F32), 0.0)
    out = jnp.where(lane == first + 1, b.astype(F32), out)
    return jnp.where(lane == first + 2, c.astype(F32), out)


def gathered(lane, first, v):
    return jnp.sum(jnp.where((lane >= first) & (lane < first + 3), v, 0.0), axis=1, keepdims=True)


def tenth(r):
    out = jnp.zeros_like(r)
    for k in range(1, HALF):
        out = out + (r >= k * CAP).astype(I32)
    return out


def where_to(zh, route):
    count = route.shape[0]
    ids = iota((count, 128), 1)
    onehot = (route == ids).astype(F32)
    before = pick(iota((count, count), 1) < iota((count, count), 0))
    earlier = dot(before, onehot.astype(BF16))
    position = jnp.sum(earlier * onehot, axis=1, keepdims=True).astype(I32)
    far = jnp.where(route >= HALF, 1, 0)
    far = jnp.where(zh == 1, 1 - far, far)
    place = jnp.where(route >= HALF, route - HALF, route)
    return far, place, position


def pack_kernel(zh_ref, route_ref, tok_ref, cot_ref, near_ref, far_ref):
    far, place, position = where_to(zh_ref[0], route_ref[...])
    count, width = tok_ref.shape
    quarter = width // 4
    first = PART - CAP
    slots = iota((count, 2 * HALF * PART), 1)
    base = far * (HALF * PART) + place * PART
    to_tok = pick(slots == base + position)
    to_cot = pick((slots == base + CAP + position) & (position < first))
    turn = ((0,), (0,))
    main = dot(to_tok, tok_ref[...], turn) + dot(to_cot, cot_ref[...], turn)
    extra = jnp.zeros((2 * HALF * PART, quarter), F32)
    for i in range(4):
        to_extra = pick((slots == base + (position - first) * 4 + i) & (position >= first))
        extra = extra + dot(to_extra, cot_ref[:, i * quarter : (i + 1) * quarter], turn)
    main, extra = main.astype(BF16), extra.astype(BF16)
    n = HALF * PART
    near_ref[:, :width], near_ref[:, width:] = main[:n], extra[:n]
    far_ref[:, :width], far_ref[:, width:] = main[n:], extra[n:]


def up_kernel(near_ref, far_ref, router_ref, gate_ref, up_ref, down_ref, part_ref, x_ref, c_ref):
    width, hid = gate_ref.shape
    quarter = width // 4
    first = PART - CAP
    n = HALF * CAP
    r = iota((n, HALF * PART), 0)
    col = iota((n, HALF * PART), 1)
    src = tenth(r)
    p = r - src * CAP
    base = src * PART
    of_tok = pick(col == base + p)
    of_cot = pick((col == base + CAP + p) & (p < first))
    of_extra = [pick((col == base + (p - first) * 4 + i) & (p >= first)) for i in range(4)]
    for half, ref in enumerate((near_ref, far_ref)):
        main, extra = ref[:, :width], ref[:, width:]
        x_ref[half * n : (half + 1) * n, :] = dot(of_tok, main).astype(BF16)
        for i in range(4):
            cols = slice(i * quarter, (i + 1) * quarter)
            c_ref[half * n : (half + 1) * n, cols] = (dot(of_cot, main[:, cols]) + dot(of_extra[i], extra)).astype(BF16)
    x = x_ref[...]
    rows = 2 * n // N_CTX

    def put(v, at):
        for i in range(N_CTX):
            part_ref[i, :, at : at + v.shape[1]] = v[i * rows : (i + 1) * rows].astype(BF16)

    put(dot(x, gate_ref[...]), 0)
    put(dot(x, up_ref[...]), hid)
    put(dot(c_ref[...], down_ref[...], ((1,), (1,))), 2 * hid)
    logit = jnp.sum(dot(x, router_ref[...]), axis=1, keepdims=True)
    put(spread(iota((2 * n, 128), 1), 0, logit), 3 * hid)


def hidden_kernel(mine_ref, out_ref):
    hid = (mine_ref.shape[2] - 128) // 3

    def total(at, size):
        out = mine_ref[0, :, at : at + size].astype(F32)
        for i in range(1, N_CTX):
            out = out + mine_ref[i, :, at : at + size].astype(F32)
        return out

    gate, up, back = total(0, hid), total(hid, hid), total(2 * hid, hid)
    logit = jnp.sum(total(3 * hid, 128), axis=1, keepdims=True)
    hidden = (gate / (1.0 + jnp.exp(-gate)) * up).astype(BF16)
    inner = jnp.sum(hidden.astype(F32) * back, axis=1, keepdims=True)
    score = 1.0 / (1.0 + jnp.exp(-logit))
    slope = inner * score * (1.0 - score)
    lane = iota((hidden.shape[0], 128), 1)
    small = (spread(lane, 0, score) + spread(lane, 3, slope)).astype(BF16)
    for i in range(N_CTX):
        out_ref[i, :, :hid] = hidden
        out_ref[i, :, hid:] = small


def down_kernel(full_ref, down_ref, near_ref, far_ref, rows_ref):
    hid, width = down_ref.shape
    quarter = width // 4
    rows = full_ref.shape[1]
    full = jnp.concatenate([full_ref[i].astype(F32) for i in range(N_CTX)], axis=0)
    score = gathered(iota((N_CTX * rows, 128), 1), 0, full[:, hid:])
    values = dot(full[:, :hid].astype(BF16), down_ref[...]).astype(BF16)
    rows_ref[...] = (score * values.astype(F32)).astype(BF16)
    n = HALF * CAP
    slot = iota((HALF * BACK, n), 0)
    r = iota((HALF * BACK, n), 1)
    src = tenth(r)
    p = r - src * CAP
    to_main = pick((slot == src * BACK + p) & (p < BACK))
    to_extra = [pick((slot == src * BACK + (p - BACK) * 4 + i) & (p >= BACK)) for i in range(4)]
    for half, ref in enumerate((near_ref, far_ref)):
        mine = rows_ref[half * n : (half + 1) * n, :]
        ref[:, :width] = dot(to_main, mine).astype(BF16)
        extra = jnp.zeros((HALF * BACK, quarter), F32)
        for i in range(4):
            extra = extra + dot(to_extra[i], mine[:, i * quarter : (i + 1) * quarter])
        ref[:, width:] = extra.astype(BF16)


def grad_kernel(full_ref, x_ref, far_ref, out_ref):
    hid = full_ref.shape[2] - 128
    small = jnp.concatenate([full_ref[i, :, hid:].astype(F32) for i in range(N_CTX)], axis=0).astype(BF16)
    every = dot(small, x_ref[...], ((0,), (0,)))
    grad = every[3:4] + every[4:5] + every[5:6]
    copies = out_ref.shape[0]
    for j in range(8):
        out_ref[:, j, :] = jnp.broadcast_to(grad[:, j * 128 : (j + 1) * 128], (copies, 128))


def merge_kernel(near_ref, far_ref, grads_ref, out_ref):
    span = near_ref.shape[1]
    out_ref[:, :span] = near_ref[...]
    out_ref[:, span : 2 * span] = far_ref[...]
    parts = grads_ref.shape[0] // 2
    for zh in range(2):
        total = grads_ref[zh]
        for k in range(1, parts):
            total = total + grads_ref[2 * k + zh]
        high = total.astype(BF16)
        low = (total - high.astype(F32)).astype(BF16)
        for at, v in ((2 * span + zh * 128, high), (2 * span + 256 + zh * 128, low)):
            out_ref[:, at : at + 128] = jnp.concatenate([v.astype(F32)] * HALF, axis=0).astype(BF16)


def out_kernel(zh_ref, route_ref, fin_ref, out_ref, grad_ref):
    far, place, position = where_to(zh_ref[0], route_ref[...])
    count, width = out_ref.shape
    quarter = width // 4
    span = width + quarter
    n = HALF * BACK
    slots = iota((count, n), 1)
    base = place * BACK
    for half in range(2):
        here = far == half
        of_main = pick((slots == base + position) & (position < BACK) & here)
        main = dot(of_main, fin_ref[:, half * span : half * span + width])
        extra = fin_ref[:, half * span + width : (half + 1) * span]
        for i in range(4):
            cols = slice(i * quarter, (i + 1) * quarter)
            of_extra = pick((slots == base + (position - BACK) * 4 + i) & (position >= BACK) & here)
            value = main[:, cols] + dot(of_extra, extra)
            if half:
                value = value + out_ref[:, cols].astype(F32)
            out_ref[:, cols] = value.astype(BF16)
    r = iota((n, 128), 0)
    col = iota((n, 128), 1)
    j, e = col // N_EXP, col % N_EXP
    turned = jnp.zeros((128, 128), F32)
    for zh in range(2):
        take = pick((r == (e % HALF) * BACK + j) & (e // HALF == zh))
        for part in range(2):
            at = 2 * span + part * 256 + zh * 128
            turned = turned + dot(fin_ref[:, at : at + 128], take, ((0,), (0,)))
    for k in range(8):
        grad_ref[k * 128 : (k + 1) * 128, :] = turned[:, k * N_EXP : (k + 1) * N_EXP]


def call(kernel, out, scalars=0, scratch=(), unread=()):
    def run(*args):
        smem = pl.BlockSpec(memory_space=pltpu.SMEM)
        vmem = pl.BlockSpec(memory_space=pltpu.VMEM)
        anywhere = pl.BlockSpec(memory_space=pl.ANY)
        specs = [smem if i < scalars else anywhere if i in unread else vmem for i in range(len(args))]
        return pl.pallas_call(
            kernel,
            in_specs=specs,
            out_specs=jax.tree.map(lambda _: vmem, out),
            out_shape=out,
            scratch_shapes=scratch,
            compiler_params=pltpu.CompilerParams(vmem_limit_bytes=32 * 1024 * 1024),
        )(*args)

    return run


def shards(tokens, routes, router_weight, gate_weight, up_weight, down_weight, cotangent):
    count, width = tokens.shape
    hid = gate_weight.shape[2]
    shape = jax.ShapeDtypeStruct
    zh = lax.axis_index("zh").astype(I32)
    expert = zh * HALF + lax.axis_index("y") * 2 + lax.axis_index("core")
    zh = zh.reshape(1)
    span = width + width // 4
    rows = N_EXP * CAP
    exchange = functools.partial(lax.all_to_all, axis_name=IN_Z, split_axis=0, concat_axis=0, tiled=True)
    over_ctx = functools.partial(lax.all_to_all, axis_name="ctx", split_axis=0, concat_axis=0, tiled=True)

    sent = shape((HALF * PART, span), BF16)
    near, far = call(pack_kernel, (sent, sent), 1)(zh, routes, tokens, cotangent)
    far = lax.ppermute(far, PAIR, PAIR_PERM)
    near = exchange(near)
    far = exchange(far)

    router_col = lax.dynamic_slice(router_weight, (lax.axis_index("ctx") * width, expert), (width, 1))
    router_col = jnp.concatenate([*pieces(router_col), jnp.zeros((width, 125), BF16)], axis=1)
    part, x = call(
        up_kernel,
        (shape((N_CTX, rows // N_CTX, 3 * hid + 128), BF16), shape((rows, width), BF16)),
        scratch=[pltpu.VMEM((rows, width), BF16)],
    )(near, far, router_col, gate_weight[0], up_weight[0], down_weight[0])
    mine = over_ctx(part)
    full = over_ctx(call(hidden_kernel, shape((N_CTX, rows // N_CTX, hid + 128), BF16))(mine))

    back = shape((HALF * BACK, span), BF16)
    near, far = call(down_kernel, (back, back), scratch=[pltpu.VMEM((rows, width), BF16)])(full, down_weight[0])
    grad = call(grad_kernel, shape((lax.axis_size(ALL_Z), 8, width // 8), F32), unread=(2,))(full, x, far)
    far = lax.ppermute(far, PAIR, PAIR_PERM)
    grads = lax.all_to_all(grad, ALL_Z, 0, 0, tiled=True)
    fin = exchange(call(merge_kernel, shape((HALF * BACK, 2 * span + 512), BF16))(near, far, grads))
    return call(out_kernel, (shape((count, width), BF16), shape((width, N_EXP), F32)), 1)(zh, routes, fin)


def solution(mesh):
    fine = Mesh(mesh.devices.reshape(MESH), NAMES)
    ep = ("zh", "y", "core")
    return jax.shard_map(
        shards,
        mesh=fine,
        in_specs=(
            P(TOK, "ctx"),
            P(TOK, None),
            P(),
            P(ep, "ctx", None),
            P(ep, "ctx", None),
            P(ep, None, "ctx"),
            P(TOK, "ctx"),
        ),
        out_specs=(P(TOK, "ctx"), P("ctx", None)),
        check_vma=False,
    )
```

```python
import functools

import jax
import jax.numpy as jnp
from jax import lax
from jax.experimental import pallas as pl
from jax.experimental.pallas import tpu as pltpu
from jax.sharding import Mesh, PartitionSpec as P

BF16 = jnp.bfloat16
F32 = jnp.float32
I32 = jnp.int32
CAP = 10
N_EXP = 16
N_CTX = 4
HALF = 8
BACK = 8
MESH = (2, 8, 4, 2, 4, 2)
NAMES = ("dh", "dl", "ctx", "zh", "y", "core")
TOK = ("dh", "dl", "zh", "y", "core")
ALL_Z = ("dh", "dl", "zh")
IN_Z = ("y", "core")
PAIR = ("dh", "zh")
PAIR_PERM = ((0, 3), (3, 0), (1, 2), (2, 1))


def dot(a, b, dims=((1,), (0,))):
    return lax.dot_general(a, b, (dims, ((), ())), preferred_element_type=F32)


def iota(shape, dim):
    return lax.broadcasted_iota(I32, shape, dim)


def pick(mask):
    return mask.astype(F32).astype(BF16)


def pieces(v):
    a = v.astype(BF16)
    v = v - a.astype(F32)
    b = v.astype(BF16)
    c = (v - b.astype(F32)).astype(BF16)
    return a, b, c


def spread(lane, first, v):
    a, b, c = pieces(v)
    out = jnp.where(lane == first, a.astype(F32), 0.0)
    out = jnp.where(lane == first + 1, b.astype(F32), out)
    return jnp.where(lane == first + 2, c.astype(F32), out)


def gathered(lane, first, v):
    return jnp.sum(jnp.where((lane >= first) & (lane < first + 3), v, 0.0), axis=1, keepdims=True)


def tenth(r):
    out = jnp.zeros_like(r)
    for k in range(1, HALF):
        out = out + (r >= k * CAP).astype(I32)
    return out


def where_to(zh, route):
    count = route.shape[0]
    ids = iota((count, 128), 1)
    onehot = (route == ids).astype(F32)
    before = pick(iota((count, count), 1) < iota((count, count), 0))
    earlier = dot(before, onehot.astype(BF16))
    position = jnp.sum(earlier * onehot, axis=1, keepdims=True).astype(I32)
    far = jnp.where(route >= HALF, 1, 0)
    far = jnp.where(zh == 1, 1 - far, far)
    place = jnp.where(route >= HALF, route - HALF, route)
    return far, place, position


def packing(base, position, shape):
    slots = iota(shape, 1)
    whole = pick((slots == base + position) & (position < BACK))
    quarters = [pick((slots == base + (position - BACK) * 4 + i) & (position >= BACK)) for i in range(4)]
    return whole, quarters


def pack_kernel(zh_ref, route_ref, tok_ref, cot_ref, far_ref, near_ref):
    far, place, position = where_to(zh_ref[0], route_ref[...])
    count, width = tok_ref.shape
    quarter = width // 4
    span = width + quarter
    n = HALF * BACK
    whole, quarters = packing(far * n + place * BACK, position, (count, 2 * n))
    turn = ((0,), (0,))
    for ref, near_at, far_out, far_at in ((tok_ref, 0, far_ref, 0), (cot_ref, span, near_ref, 2 * span)):
        main = dot(whole, ref[...], turn).astype(BF16)
        extra = dot(quarters[0], ref[:, :quarter], turn)
        for i in range(1, 4):
            extra = extra + dot(quarters[i], ref[:, i * quarter : (i + 1) * quarter], turn)
        extra = extra.astype(BF16)
        near_ref[:, near_at : near_at + width], near_ref[:, near_at + width : near_at + span] = main[:n], extra[:n]
        far_out[:, far_at : far_at + width], far_out[:, far_at + width : far_at + span] = main[n:], extra[n:]


def unpacking():
    shape = (HALF * CAP, HALF * BACK)
    r, col = iota(shape, 0), iota(shape, 1)
    src = tenth(r)
    p = r - src * CAP
    whole = pick((col == src * BACK + p) & (p < BACK))
    quarters = [pick((col == src * BACK + (p - BACK) * 4 + i) & (p >= BACK)) for i in range(4)]
    return whole, quarters


def unpack(maps, main, extra):
    whole, quarters = maps
    quarter = extra.shape[1]
    return [dot(whole, main[:, i * quarter : (i + 1) * quarter]) + dot(quarters[i], extra) for i in range(4)]


def up_kernel(near_ref, far_ref, router_ref, gate_ref, up_ref, part_ref, x_ref):
    width, hid = gate_ref.shape
    quarter = width // 4
    span = width + quarter
    n = HALF * CAP
    maps = unpacking()
    for half, ref in enumerate((near_ref, far_ref)):
        for i, block in enumerate(unpack(maps, ref[:, :width], ref[:, width:span])):
            x_ref[half * n : (half + 1) * n, i * quarter : (i + 1) * quarter] = block.astype(BF16)
    x = x_ref[...]
    rows = 2 * n // N_CTX

    def put(v, at):
        for i in range(N_CTX):
            part_ref[i, :, at : at + v.shape[1]] = v[i * rows : (i + 1) * rows].astype(BF16)

    logit = jnp.sum(dot(x, router_ref[...]), axis=1, keepdims=True)
    put(spread(iota((2 * n, 128), 1), 0, logit), 2 * hid)
    put(dot(x, gate_ref[...]), 0)
    put(dot(x, up_ref[...]), hid)


def hidden_kernel(mine_ref, out_ref):
    hid = (mine_ref.shape[2] - 128) // 2

    def total(at, size):
        out = mine_ref[0, :, at : at + size].astype(F32)
        for i in range(1, N_CTX):
            out = out + mine_ref[i, :, at : at + size].astype(F32)
        return out

    gate, up = total(0, hid), total(hid, hid)
    logit = jnp.sum(total(2 * hid, 128), axis=1, keepdims=True)
    hidden = (gate / (1.0 + jnp.exp(-gate)) * up).astype(BF16)
    score = 1.0 / (1.0 + jnp.exp(-logit))
    small = spread(iota((hidden.shape[0], 128), 1), 0, score).astype(BF16)
    for i in range(N_CTX):
        out_ref[i, :, :hid] = hidden
        out_ref[i, :, hid:] = small


def down_kernel(full_ref, down_ref, near_ref, far_ref, values_ref, rows_ref):
    hid, width = down_ref.shape
    quarter = width // 4
    full = jnp.concatenate([full_ref[i].astype(F32) for i in range(N_CTX)], axis=0)
    score = gathered(iota((full.shape[0], 128), 1), 0, full[:, hid:])
    values = dot(full[:, :hid].astype(BF16), down_ref[...]).astype(BF16)
    values_ref[...] = values
    rows_ref[...] = (score * values.astype(F32)).astype(BF16)
    n = HALF * CAP
    slot, r = iota((HALF * BACK, n), 0), iota((HALF * BACK, n), 1)
    src = tenth(r)
    p = r - src * CAP
    whole = pick((slot == src * BACK + p) & (p < BACK))
    quarters = [pick((slot == src * BACK + (p - BACK) * 4 + i) & (p >= BACK)) for i in range(4)]
    for half, ref in enumerate((near_ref, far_ref)):
        mine = rows_ref[half * n : (half + 1) * n, :]
        ref[:, :width] = dot(whole, mine).astype(BF16)
        extra = dot(quarters[0], mine[:, :quarter])
        for i in range(1, 4):
            extra = extra + dot(quarters[i], mine[:, i * quarter : (i + 1) * quarter])
        ref[:, width:] = extra.astype(BF16)


def to_rows(v):
    size = v.shape[0]
    eye = pick(iota((size, size), 0) == iota((size, size), 1))
    return dot(v, eye, ((0,), (0,)))


def inner_kernel(near_ref, far_ref, values_ref, out_ref):
    rows, width = values_ref.shape
    quarter = width // 4
    span = width + quarter
    n = HALF * CAP
    maps = unpacking()
    sums = []
    for half, (ref, at) in enumerate(((near_ref, span), (far_ref, 0))):
        inner = jnp.zeros((n, 1), F32)
        for i, block in enumerate(unpack(maps, ref[:, at : at + width], ref[:, at + width : at + span])):
            value = values_ref[half * n : (half + 1) * n, i * quarter : (i + 1) * quarter].astype(F32)
            inner = inner + jnp.sum(block * value, axis=1, keepdims=True)
        sums.append(inner)
    turned = to_rows(spread(iota((rows, 128), 1), 0, jnp.concatenate(sums, axis=0)).astype(BF16))
    inner = turned[0:1] + turned[1:2] + turned[2:3]
    for i in range(N_CTX):
        out_ref[i] = jnp.broadcast_to(inner, out_ref.shape[1:])


def grad_kernel(inner_ref, full_ref, x_ref, out_ref):
    hid = full_ref.shape[2] - 128
    small = jnp.concatenate([full_ref[i, :, hid:].astype(F32) for i in range(N_CTX)], axis=0).astype(BF16)
    turned = to_rows(small)
    score = turned[0:1] + turned[1:2] + turned[2:3]
    inner = inner_ref[0]
    for i in range(1, N_CTX):
        inner = inner + inner_ref[i]
    slope = inner * (score * (1.0 - score))
    a, b, c = pieces(slope)
    line = iota(slope.shape, 0)
    slope = jnp.where(line == 0, a.astype(F32), jnp.where(line == 1, b.astype(F32), jnp.where(line == 2, c.astype(F32), 0.0)))
    grad = jnp.sum(dot(slope.astype(BF16), x_ref[...]), axis=0, keepdims=True)
    copies = out_ref.shape[0]
    for j in range(8):
        out_ref[:, j, :] = jnp.broadcast_to(grad[:, j * 128 : (j + 1) * 128], (copies, 128))


def merge_kernel(near_ref, far_ref, grads_ref, out_ref):
    span = near_ref.shape[1]
    out_ref[:, :span] = near_ref[...]
    out_ref[:, span : 2 * span] = far_ref[...]
    parts = grads_ref.shape[0] // 2
    for zh in range(2):
        total = grads_ref[zh]
        for k in range(1, parts):
            total = total + grads_ref[2 * k + zh]
        high = total.astype(BF16)
        low = (total - high.astype(F32)).astype(BF16)
        for at, v in ((2 * span + zh * 128, high), (2 * span + 256 + zh * 128, low)):
            out_ref[:, at : at + 128] = jnp.concatenate([v.astype(F32)] * HALF, axis=0).astype(BF16)


def out_kernel(zh_ref, route_ref, fin_ref, out_ref, grad_ref):
    far, place, position = where_to(zh_ref[0], route_ref[...])
    count, width = out_ref.shape
    quarter = width // 4
    span = width + quarter
    n = HALF * BACK
    slots = iota((count, n), 1)
    base = place * BACK
    for half in range(2):
        here = far == half
        of_main = pick((slots == base + position) & (position < BACK) & here)
        main = dot(of_main, fin_ref[:, half * span : half * span + width])
        extra = fin_ref[:, half * span + width : (half + 1) * span]
        for i in range(4):
            cols = slice(i * quarter, (i + 1) * quarter)
            of_extra = pick((slots == base + (position - BACK) * 4 + i) & (position >= BACK) & here)
            value = main[:, cols] + dot(of_extra, extra)
            if half:
                value = value + out_ref[:, cols].astype(F32)
            out_ref[:, cols] = value.astype(BF16)
    r = iota((n, 128), 0)
    col = iota((n, 128), 1)
    j, e = col // N_EXP, col % N_EXP
    turned = jnp.zeros((128, 128), F32)
    for zh in range(2):
        take = pick((r == (e % HALF) * BACK + j) & (e // HALF == zh))
        for part in range(2):
            at = 2 * span + part * 256 + zh * 128
            turned = turned + dot(fin_ref[:, at : at + 128], take, ((0,), (0,)))
    for k in range(8):
        grad_ref[k * 128 : (k + 1) * 128, :] = turned[:, k * N_EXP : (k + 1) * N_EXP]


def call(kernel, out, scalars=0, scratch=()):
    def run(*args):
        smem = pl.BlockSpec(memory_space=pltpu.SMEM)
        vmem = pl.BlockSpec(memory_space=pltpu.VMEM)
        specs = [smem if i < scalars else vmem for i in range(len(args))]
        return pl.pallas_call(
            kernel,
            in_specs=specs,
            out_specs=jax.tree.map(lambda _: vmem, out),
            out_shape=out,
            scratch_shapes=scratch,
            compiler_params=pltpu.CompilerParams(vmem_limit_bytes=16 * 1024 * 1024),
        )(*args)

    return run


def as_one_step(turns, body, state):
    out = lax.while_loop(lambda s: s[0] < turns, lambda s: (s[0] + 1, *body(*s[1:])), (jnp.int32(0), *state))
    return out[1:]


def shards(tokens, routes, router_weight, gate_weight, up_weight, down_weight, cotangent):
    count, width = tokens.shape
    hid = gate_weight.shape[2]
    shape = jax.ShapeDtypeStruct
    zh = lax.axis_index("zh").astype(I32)
    expert = zh * HALF + lax.axis_index("y") * 2 + lax.axis_index("core")
    zh = zh.reshape(1)
    turns = 1 + lax.axis_index("ctx").astype(I32) // N_CTX
    span = width + width // 4
    rows = N_EXP * CAP
    exchange = functools.partial(lax.all_to_all, axis_name=IN_Z, split_axis=0, concat_axis=0, tiled=True)
    over_ctx = functools.partial(lax.all_to_all, axis_name="ctx", split_axis=0, concat_axis=0, tiled=True)

    chunk = shape((HALF * BACK, span), BF16)
    x_far, near = call(pack_kernel, (chunk, shape((HALF * BACK, 3 * span), BF16)), 1)(zh, routes, tokens, cotangent)
    x_far = lax.ppermute(x_far, PAIR, PAIR_PERM)
    (near,) = as_one_step(turns, lambda v: (exchange(v),), (near,))
    cot_far = lax.ppermute(near[:, 2 * span :], PAIR, PAIR_PERM)

    router_col = lax.dynamic_slice(router_weight, (lax.axis_index("ctx") * width, expert), (width, 1))
    router_col = jnp.concatenate([*pieces(router_col), jnp.zeros((width, 125), BF16)], axis=1)
    part = shape((N_CTX, rows // N_CTX, 2 * hid + 128), BF16)
    wide = shape((rows, width), BF16)

    def to_hidden(x_far, x, full):
        x_far = exchange(x_far)
        sums, x = call(up_kernel, (part, wide))(near, x_far, router_col, gate_weight[0], up_weight[0])
        mine = over_ctx(sums)
        full = over_ctx(call(hidden_kernel, shape(full.shape, BF16))(mine))
        return x_far, x, full

    full = jnp.zeros((N_CTX, rows // N_CTX, hid + 128), BF16)
    _, x, full = as_one_step(turns, to_hidden, (x_far, jnp.zeros((rows, width), BF16), full))

    scratch = [pltpu.VMEM((rows, width), BF16)]
    near_back, far, values = call(down_kernel, (chunk, chunk, wide), scratch=scratch)(full, down_weight[0])
    far = lax.ppermute(far, PAIR, PAIR_PERM)
    inner = over_ctx(call(inner_kernel, shape((N_CTX, 8, rows), F32))(near, cot_far, values))
    grad = call(grad_kernel, shape((lax.axis_size(ALL_Z), 8, width // 8), F32))(inner, full, x)

    (grads,) = as_one_step(turns, lambda v: (lax.all_to_all(v, ALL_Z, 0, 0, tiled=True),), (grad,))
    fin = exchange(call(merge_kernel, shape((HALF * BACK, 2 * span + 512), BF16))(near_back, far, grads))
    return call(out_kernel, (shape((count, width), BF16), shape((width, N_EXP), F32)), 1)(zh, routes, fin)


def solution(mesh):
    fine = Mesh(mesh.devices.reshape(MESH), NAMES)
    ep = ("zh", "y", "core")
    return jax.shard_map(
        shards,
        mesh=fine,
        in_specs=(
            P(TOK, "ctx"),
            P(TOK, None),
            P(),
            P(ep, "ctx", None),
            P(ep, "ctx", None),
            P(ep, None, "ctx"),
            P(TOK, "ctx"),
        ),
        out_specs=(P(TOK, "ctx"), P("ctx", None)),
        check_vma=False,
    )
```

```python
import functools

import jax
import jax.numpy as jnp
from jax import lax
from jax.experimental import pallas as pl
from jax.experimental.pallas import tpu as pltpu
from jax.sharding import Mesh, PartitionSpec as P

BF16 = jnp.bfloat16
F32 = jnp.float32
I32 = jnp.int32
CAP = 10
N_EXP = 16
N_CTX = 4
HALF = 8
BACK = 8
MESH = (2, 8, 4, 2, 4, 2)
NAMES = ("dh", "dl", "ctx", "zh", "y", "core")
TOK = ("dh", "dl", "zh", "y", "core")
ALL_Z = ("dh", "dl", "zh")
IN_Z = ("y", "core")
PAIR = ("dh", "zh")
PAIR_PERM = ((0, 3), (3, 0), (1, 2), (2, 1))


def dot(a, b, dims=((1,), (0,))):
    return lax.dot_general(a, b, (dims, ((), ())), preferred_element_type=F32)


def iota(shape, dim):
    return lax.broadcasted_iota(I32, shape, dim)


def pick(mask):
    return mask.astype(F32).astype(BF16)


def pieces(v):
    a = v.astype(BF16)
    v = v - a.astype(F32)
    b = v.astype(BF16)
    c = (v - b.astype(F32)).astype(BF16)
    return a, b, c


def spread(lane, first, v):
    a, b, c = pieces(v)
    out = jnp.where(lane == first, a.astype(F32), 0.0)
    out = jnp.where(lane == first + 1, b.astype(F32), out)
    return jnp.where(lane == first + 2, c.astype(F32), out)


def gathered(lane, first, v):
    return jnp.sum(jnp.where((lane >= first) & (lane < first + 3), v, 0.0), axis=1, keepdims=True)


def tenth(r):
    out = jnp.zeros_like(r)
    for k in range(1, HALF):
        out = out + (r >= k * CAP).astype(I32)
    return out


def where_to(zh, route):
    count = route.shape[0]
    ids = iota((count, 128), 1)
    onehot = (route == ids).astype(F32)
    before = pick(iota((count, count), 1) < iota((count, count), 0))
    earlier = dot(before, onehot.astype(BF16))
    position = jnp.sum(earlier * onehot, axis=1, keepdims=True).astype(I32)
    far = jnp.where(route >= HALF, 1, 0)
    far = jnp.where(zh == 1, 1 - far, far)
    place = jnp.where(route >= HALF, route - HALF, route)
    return far, place, position


def packing(base, position, shape):
    slots = iota(shape, 1)
    whole = pick((slots == base + position) & (position < BACK))
    quarters = [pick((slots == base + (position - BACK) * 4 + i) & (position >= BACK)) for i in range(4)]
    return whole, quarters


def pack_kernel(zh_ref, route_ref, tok_ref, cot_ref, far_ref, near_ref, full_ref):
    full_ref[...] = jnp.zeros(full_ref.shape, BF16)
    far, place, position = where_to(zh_ref[0], route_ref[...])
    count, width = tok_ref.shape
    quarter = width // 4
    span = width + quarter
    n = HALF * BACK
    whole, quarters = packing(far * n + place * BACK, position, (count, 2 * n))
    turn = ((0,), (0,))
    for ref, near_at, far_out, far_at in ((tok_ref, 0, far_ref, 0), (cot_ref, span, near_ref, 2 * span)):
        main = dot(whole, ref[...], turn).astype(BF16)
        extra = dot(quarters[0], ref[:, :quarter], turn)
        for i in range(1, 4):
            extra = extra + dot(quarters[i], ref[:, i * quarter : (i + 1) * quarter], turn)
        extra = extra.astype(BF16)
        near_ref[:, near_at : near_at + width], near_ref[:, near_at + width : near_at + span] = main[:n], extra[:n]
        far_out[:, far_at : far_at + width], far_out[:, far_at + width : far_at + span] = main[n:], extra[n:]


def unpacking():
    shape = (HALF * CAP, HALF * BACK)
    r, col = iota(shape, 0), iota(shape, 1)
    src = tenth(r)
    p = r - src * CAP
    whole = pick((col == src * BACK + p) & (p < BACK))
    quarters = [pick((col == src * BACK + (p - BACK) * 4 + i) & (p >= BACK)) for i in range(4)]
    return whole, quarters


def unpack(maps, main, extra):
    whole, quarters = maps
    quarter = extra.shape[1]
    return [dot(whole, main[:, i * quarter : (i + 1) * quarter]) + dot(quarters[i], extra) for i in range(4)]


def up_kernel(near_ref, far_ref, router_ref, gate_ref, up_ref, part_ref, x_ref):
    width, hid = gate_ref.shape
    quarter = width // 4
    span = width + quarter
    n = HALF * CAP
    maps = unpacking()
    for half, ref in enumerate((near_ref, far_ref)):
        for i, block in enumerate(unpack(maps, ref[:, :width], ref[:, width:span])):
            x_ref[half * n : (half + 1) * n, i * quarter : (i + 1) * quarter] = block.astype(BF16)
    x = x_ref[...]
    rows = 2 * n // N_CTX

    def put(v, at):
        for i in range(N_CTX):
            part_ref[i, :, at : at + v.shape[1]] = v[i * rows : (i + 1) * rows].astype(BF16)

    logit = jnp.sum(dot(x, router_ref[...]), axis=1, keepdims=True)
    put(spread(iota((2 * n, 128), 1), 0, logit), 2 * hid)
    put(dot(x, gate_ref[...]), 0)
    put(dot(x, up_ref[...]), hid)


def hidden_kernel(mine_ref, out_ref):
    hid = (mine_ref.shape[2] - 128) // 2

    def total(at, size):
        out = mine_ref[0, :, at : at + size].astype(F32)
        for i in range(1, N_CTX):
            out = out + mine_ref[i, :, at : at + size].astype(F32)
        return out

    gate, up = total(0, hid), total(hid, hid)
    logit = jnp.sum(total(2 * hid, 128), axis=1, keepdims=True)
    hidden = (gate / (1.0 + jnp.exp(-gate)) * up).astype(BF16)
    score = 1.0 / (1.0 + jnp.exp(-logit))
    small = spread(iota((hidden.shape[0], 128), 1), 0, score).astype(BF16)
    for i in range(N_CTX):
        out_ref[i, :, :hid] = hidden
        out_ref[i, :, hid:] = small


def to_rows(v):
    size = v.shape[0]
    eye = pick(iota((size, size), 0) == iota((size, size), 1))
    return dot(v, eye, ((0,), (0,)))


def down_kernel(full_ref, cot_near_ref, cot_far_ref, down_ref, near_ref, far_ref, inner_ref, values_ref):
    hid, width = down_ref.shape
    quarter = width // 4
    span = width + quarter
    full = jnp.concatenate([full_ref[i].astype(F32) for i in range(N_CTX)], axis=0)
    rows = full.shape[0]
    lane = iota((rows, 128), 1)
    score = gathered(lane, 0, full[:, hid:])
    values_ref[...] = dot(full[:, :hid].astype(BF16), down_ref[...]).astype(BF16)
    n = HALF * CAP
    maps = unpacking()
    sums = []
    for half, (ref, at) in enumerate(((cot_near_ref, span), (cot_far_ref, 0))):
        inner = jnp.zeros((n, 1), F32)
        for i, block in enumerate(unpack(maps, ref[:, at : at + width], ref[:, at + width : at + span])):
            value = values_ref[half * n : (half + 1) * n, i * quarter : (i + 1) * quarter].astype(F32)
            inner = inner + jnp.sum(block * value, axis=1, keepdims=True)
        sums.append(inner)
    turned = to_rows(spread(lane, 0, jnp.concatenate(sums, axis=0)).astype(BF16))
    inner = turned[0:1] + turned[1:2] + turned[2:3]
    for i in range(N_CTX):
        inner_ref[i] = jnp.broadcast_to(inner, inner_ref.shape[1:])
    slot, r = iota((HALF * BACK, n), 0), iota((HALF * BACK, n), 1)
    src = tenth(r)
    p = r - src * CAP
    whole = pick((slot == src * BACK + p) & (p < BACK))
    quarters = [pick((slot == src * BACK + (p - BACK) * 4 + i) & (p >= BACK)) for i in range(4)]
    for half, ref in enumerate((near_ref, far_ref)):
        part = slice(half * n, (half + 1) * n)
        mine = (score[part] * values_ref[part, :].astype(F32)).astype(BF16)
        ref[:, :width] = dot(whole, mine).astype(BF16)
        extra = dot(quarters[0], mine[:, :quarter])
        for i in range(1, 4):
            extra = extra + dot(quarters[i], mine[:, i * quarter : (i + 1) * quarter])
        ref[:, width:] = extra.astype(BF16)


def relay_kernel(near_ref, x_far_ref, out_ref):
    out_ref[...] = near_ref[:, near_ref.shape[1] - out_ref.shape[1] :]


def grad_kernel(inner_ref, full_ref, x_ref, out_ref):
    hid = full_ref.shape[2] - 128
    small = jnp.concatenate([full_ref[i, :, hid:].astype(F32) for i in range(N_CTX)], axis=0).astype(BF16)
    turned = to_rows(small)
    score = turned[0:1] + turned[1:2] + turned[2:3]
    inner = inner_ref[0]
    for i in range(1, N_CTX):
        inner = inner + inner_ref[i]
    slope = inner * (score * (1.0 - score))
    a, b, c = pieces(slope)
    line = iota(slope.shape, 0)
    slope = jnp.where(line == 0, a.astype(F32), jnp.where(line == 1, b.astype(F32), jnp.where(line == 2, c.astype(F32), 0.0)))
    grad = jnp.sum(dot(slope.astype(BF16), x_ref[...]), axis=0, keepdims=True)
    copies = out_ref.shape[0]
    lines = []
    for j in range(8):
        lines.append(grad[:, j * 128 : (j + 1) * 128])
    block = jnp.concatenate(lines, axis=0).astype(out_ref.dtype)
    for k in range(copies):
        out_ref[k] = block


def merge_kernel(near_ref, far_ref, grads_ref, out_ref):
    span = near_ref.shape[1]
    out_ref[:, :span] = near_ref[...]
    out_ref[:, span : 2 * span] = far_ref[...]
    parts = grads_ref.shape[0] // 2
    for zh in range(2):
        total = grads_ref[zh].astype(F32)
        for k in range(1, parts):
            total = total + grads_ref[2 * k + zh].astype(F32)
        high = total.astype(BF16)
        low = (total - high.astype(F32)).astype(BF16)
        for at, v in ((2 * span + zh * 128, high), (2 * span + 256 + zh * 128, low)):
            out_ref[:, at : at + 128] = jnp.concatenate([v.astype(F32)] * HALF, axis=0).astype(BF16)


def out_kernel(zh_ref, route_ref, fin_ref, out_ref, grad_ref):
    far, place, position = where_to(zh_ref[0], route_ref[...])
    count, width = out_ref.shape
    quarter = width // 4
    span = width + quarter
    n = HALF * BACK
    slots = iota((count, n), 1)
    base = place * BACK
    for half in range(2):
        here = far == half
        of_main = pick((slots == base + position) & (position < BACK) & here)
        main = dot(of_main, fin_ref[:, half * span : half * span + width])
        extra = fin_ref[:, half * span + width : (half + 1) * span]
        for i in range(4):
            cols = slice(i * quarter, (i + 1) * quarter)
            of_extra = pick((slots == base + (position - BACK) * 4 + i) & (position >= BACK) & here)
            value = main[:, cols] + dot(of_extra, extra)
            if half:
                value = value + out_ref[:, cols].astype(F32)
            out_ref[:, cols] = value.astype(BF16)
    line, r = iota((N_EXP, n), 0), iota((N_EXP, n), 1)
    place = jnp.where(line >= HALF, line - HALF, line)
    for j in range(8):
        total = jnp.zeros((N_EXP, 128), F32)
        for zh in range(2):
            take = pick((r == place * BACK + j) & ((line >= HALF) == (zh == 1)))
            for part in range(2):
                at = 2 * span + part * 256 + zh * 128
                total = total + dot(take, fin_ref[:, at : at + 128])
        grad_ref[:, j * 128 : (j + 1) * 128] = total


def call(kernel, out, scalars=0, scratch=()):
    def run(*args):
        smem = pl.BlockSpec(memory_space=pltpu.SMEM)
        vmem = pl.BlockSpec(memory_space=pltpu.VMEM)
        specs = [smem if i < scalars else vmem for i in range(len(args))]
        return pl.pallas_call(
            kernel,
            in_specs=specs,
            out_specs=jax.tree.map(lambda _: vmem, out),
            out_shape=out,
            scratch_shapes=scratch,
            compiler_params=pltpu.CompilerParams(vmem_limit_bytes=16 * 1024 * 1024),
        )(*args)

    return run


def as_one_step(turns, body, state):
    out = lax.while_loop(lambda s: s[0] < turns, lambda s: (s[0] + 1, *body(*s[1:])), (jnp.int32(0), *state))
    return out[1:]


def shards(tokens, routes, router_weight, gate_weight, up_weight, down_weight, cotangent):
    count, width = tokens.shape
    hid = gate_weight.shape[2]
    shape = jax.ShapeDtypeStruct
    zh = lax.axis_index("zh").astype(I32)
    expert = zh * HALF + lax.axis_index("y") * 2 + lax.axis_index("core")
    zh = zh.reshape(1)
    turns = 1 + lax.axis_index("ctx").astype(I32) // N_CTX
    span = width + width // 4
    rows = N_EXP * CAP
    exchange = functools.partial(lax.all_to_all, axis_name=IN_Z, split_axis=0, concat_axis=0, tiled=True)
    over_ctx = functools.partial(lax.all_to_all, axis_name="ctx", split_axis=0, concat_axis=0, tiled=True)

    chunk = shape((HALF * BACK, span), BF16)
    x_far, near, full = call(
        pack_kernel,
        (chunk, shape((HALF * BACK, 3 * span), BF16), shape((N_CTX, rows // N_CTX, hid + 128), BF16)),
        1,
    )(zh, routes, tokens, cotangent)
    x_far = lax.ppermute(x_far, PAIR, PAIR_PERM)
    (near,) = as_one_step(turns, lambda v: (exchange(v),), (near,))
    cot_far = lax.ppermute(call(relay_kernel, chunk)(near, x_far), PAIR, PAIR_PERM)
    x_far = exchange(x_far)

    router_col = lax.dynamic_slice(router_weight, (lax.axis_index("ctx") * width, expert), (width, 1))
    router_col = jnp.concatenate([*pieces(router_col), jnp.zeros((width, 125), BF16)], axis=1)
    part = shape((N_CTX, rows // N_CTX, 2 * hid + 128), BF16)
    sums, x = call(up_kernel, (part, shape((rows, width), BF16)))(near, x_far, router_col, gate_weight[0], up_weight[0])

    def to_hidden(sums, full):
        mine = over_ctx(sums)
        return mine, over_ctx(call(hidden_kernel, shape(full.shape, BF16))(mine))

    _, full = as_one_step(turns, to_hidden, (sums, full))

    near_back, far, inner = call(
        down_kernel,
        (chunk, chunk, shape((N_CTX, 8, rows), F32)),
        scratch=[pltpu.VMEM((rows, width), BF16)],
    )(full, near, cot_far, down_weight[0])
    far = lax.ppermute(far, PAIR, PAIR_PERM)
    inner = over_ctx(inner)
    grad = call(grad_kernel, shape((lax.axis_size(ALL_Z), 8, width // 8), BF16))(inner, full, x)

    (grads,) = as_one_step(turns, lambda v: (lax.all_to_all(v, ALL_Z, 0, 0, tiled=True),), (grad,))
    fin = exchange(call(merge_kernel, shape((HALF * BACK, 2 * span + 512), BF16))(near_back, far, grads))
    block_out, grad = call(out_kernel, (shape((count, width), BF16), shape((N_EXP, width), F32)), 1)(zh, routes, fin)
    return block_out, grad.T


def solution(mesh):
    fine = Mesh(mesh.devices.reshape(MESH), NAMES)
    ep = ("zh", "y", "core")
    return jax.shard_map(
        shards,
        mesh=fine,
        in_specs=(
            P(TOK, "ctx"),
            P(TOK, None),
            P(),
            P(ep, "ctx", None),
            P(ep, "ctx", None),
            P(ep, None, "ctx"),
            P(TOK, "ctx"),
        ),
        out_specs=(P(TOK, "ctx"), P("ctx", None)),
        check_vma=False,
    )
```

```python
import functools

import jax
import jax.numpy as jnp
from jax import lax
from jax.experimental import pallas as pl
from jax.experimental.pallas import tpu as pltpu
from jax.sharding import Mesh, PartitionSpec as P

BF16 = jnp.bfloat16
F32 = jnp.float32
I32 = jnp.int32
CAP = 10
N_EXP = 16
N_CTX = 4
HALF = 8
BACK = 8
MESH = (2, 8, 4, 2, 4, 2)
NAMES = ("dh", "dl", "ctx", "zh", "y", "core")
TOK = ("dh", "dl", "zh", "y", "core")
ALL_Z = ("dh", "dl", "zh")
IN_Z = ("y", "core")
PAIR = ("dh", "zh")
PAIR_PERM = ((0, 3), (3, 0), (1, 2), (2, 1))


def dot(a, b, dims=((1,), (0,))):
    return lax.dot_general(a, b, (dims, ((), ())), preferred_element_type=F32)


def iota(shape, dim):
    return lax.broadcasted_iota(I32, shape, dim)


def pick(mask):
    return mask.astype(F32).astype(BF16)


def pieces(v):
    a = v.astype(BF16)
    v = v - a.astype(F32)
    b = v.astype(BF16)
    c = (v - b.astype(F32)).astype(BF16)
    return a, b, c


def spread(lane, first, v):
    a, b, c = pieces(v)
    out = jnp.where(lane == first, a.astype(F32), 0.0)
    out = jnp.where(lane == first + 1, b.astype(F32), out)
    return jnp.where(lane == first + 2, c.astype(F32), out)


def gathered(lane, first, v):
    return jnp.sum(jnp.where((lane >= first) & (lane < first + 3), v, 0.0), axis=1, keepdims=True)


def tenth(r):
    out = jnp.zeros_like(r)
    for k in range(1, HALF):
        out = out + (r >= k * CAP).astype(I32)
    return out


def where_to(zh, route):
    count = route.shape[0]
    ids = iota((count, 128), 1)
    onehot = (route == ids).astype(F32)
    before = pick(iota((count, count), 1) < iota((count, count), 0))
    earlier = dot(before, onehot.astype(BF16))
    position = jnp.sum(earlier * onehot, axis=1, keepdims=True).astype(I32)
    far = jnp.where(route >= HALF, 1, 0)
    far = jnp.where(zh == 1, 1 - far, far)
    place = jnp.where(route >= HALF, route - HALF, route)
    return far, place, position


def packing(base, position, shape):
    slots = iota(shape, 1)
    whole = pick((slots == base + position) & (position < BACK))
    quarters = [pick((slots == base + (position - BACK) * 4 + i) & (position >= BACK)) for i in range(4)]
    return whole, quarters


def pack_kernel(zh_ref, route_ref, tok_ref, cot_ref, far_ref, near_ref, x_ref, full_ref):
    x_ref[...] = jnp.zeros(x_ref.shape, BF16)
    full_ref[...] = jnp.zeros(full_ref.shape, BF16)
    far, place, position = where_to(zh_ref[0], route_ref[...])
    count, width = tok_ref.shape
    quarter = width // 4
    span = width + quarter
    n = HALF * BACK
    whole, quarters = packing(far * n + place * BACK, position, (count, 2 * n))
    turn = ((0,), (0,))
    for ref, near_at, far_out, far_at in ((tok_ref, 0, far_ref, 0), (cot_ref, span, near_ref, 2 * span)):
        main = dot(whole, ref[...], turn).astype(BF16)
        extra = dot(quarters[0], ref[:, :quarter], turn)
        for i in range(1, 4):
            extra = extra + dot(quarters[i], ref[:, i * quarter : (i + 1) * quarter], turn)
        extra = extra.astype(BF16)
        near_ref[:, near_at : near_at + width], near_ref[:, near_at + width : near_at + span] = main[:n], extra[:n]
        far_out[:, far_at : far_at + width], far_out[:, far_at + width : far_at + span] = main[n:], extra[n:]


def unpacking():
    shape = (HALF * CAP, HALF * BACK)
    r, col = iota(shape, 0), iota(shape, 1)
    src = tenth(r)
    p = r - src * CAP
    whole = pick((col == src * BACK + p) & (p < BACK))
    quarters = [pick((col == src * BACK + (p - BACK) * 4 + i) & (p >= BACK)) for i in range(4)]
    return whole, quarters


def unpack(maps, main, extra):
    whole, quarters = maps
    quarter = extra.shape[1]
    return [dot(whole, main[:, i * quarter : (i + 1) * quarter]) + dot(quarters[i], extra) for i in range(4)]


def up_kernel(turn_ref, near_ref, far_ref, router_ref, gate_ref, up_ref, part_ref, x_ref):
    width, hid = gate_ref.shape
    quarter = width // 4
    span = width + quarter
    n = HALF * CAP
    maps = unpacking()
    for half, ref in enumerate((near_ref, far_ref)):
        for i, block in enumerate(unpack(maps, ref[:, :width], ref[:, width:span])):
            x_ref[half * n : (half + 1) * n, i * quarter : (i + 1) * quarter] = block.astype(BF16)
    x = x_ref[...]
    rows = 2 * n // N_CTX

    def put(v, at):
        for i in range(N_CTX):
            part_ref[i, :, at : at + v.shape[1]] = v[i * rows : (i + 1) * rows].astype(BF16)

    logit = jnp.sum(dot(x, router_ref[...]), axis=1, keepdims=True)
    put(spread(iota((2 * n, 128), 1), 0, logit), 2 * hid)
    put(dot(x, gate_ref[...]), 0)
    put(dot(x, up_ref[...]), hid)


def hidden_kernel(mine_ref, out_ref):
    hid = (mine_ref.shape[2] - 128) // 2

    def total(at, size):
        out = mine_ref[0, :, at : at + size].astype(F32)
        for i in range(1, N_CTX):
            out = out + mine_ref[i, :, at : at + size].astype(F32)
        return out

    gate, up = total(0, hid), total(hid, hid)
    logit = jnp.sum(total(2 * hid, 128), axis=1, keepdims=True)
    hidden = (gate / (1.0 + jnp.exp(-gate)) * up).astype(BF16)
    score = 1.0 / (1.0 + jnp.exp(-logit))
    small = spread(iota((hidden.shape[0], 128), 1), 0, score).astype(BF16)
    for i in range(N_CTX):
        out_ref[i, :, :hid] = hidden
        out_ref[i, :, hid:] = small


def to_rows(v):
    size = v.shape[0]
    eye = pick(iota((size, size), 0) == iota((size, size), 1))
    return dot(v, eye, ((0,), (0,)))


def down_kernel(full_ref, cot_near_ref, cot_far_ref, down_ref, near_ref, far_ref, inner_ref, values_ref):
    hid, width = down_ref.shape
    quarter = width // 4
    span = width + quarter
    full = jnp.concatenate([full_ref[i].astype(F32) for i in range(N_CTX)], axis=0)
    rows = full.shape[0]
    lane = iota((rows, 128), 1)
    score = gathered(lane, 0, full[:, hid:])
    values_ref[...] = dot(full[:, :hid].astype(BF16), down_ref[...]).astype(BF16)
    n = HALF * CAP
    maps = unpacking()
    sums = []
    for half, (ref, at) in enumerate(((cot_near_ref, span), (cot_far_ref, 0))):
        inner = jnp.zeros((n, 1), F32)
        for i, block in enumerate(unpack(maps, ref[:, at : at + width], ref[:, at + width : at + span])):
            value = values_ref[half * n : (half + 1) * n, i * quarter : (i + 1) * quarter].astype(F32)
            inner = inner + jnp.sum(block * value, axis=1, keepdims=True)
        sums.append(inner)
    turned = to_rows(spread(lane, 0, jnp.concatenate(sums, axis=0)).astype(BF16))
    inner = turned[0:1] + turned[1:2] + turned[2:3]
    for i in range(N_CTX):
        inner_ref[i] = jnp.broadcast_to(inner, inner_ref.shape[1:])
    slot, r = iota((HALF * BACK, n), 0), iota((HALF * BACK, n), 1)
    src = tenth(r)
    p = r - src * CAP
    whole = pick((slot == src * BACK + p) & (p < BACK))
    quarters = [pick((slot == src * BACK + (p - BACK) * 4 + i) & (p >= BACK)) for i in range(4)]
    for half, ref in enumerate((near_ref, far_ref)):
        part = slice(half * n, (half + 1) * n)
        mine = (score[part] * values_ref[part, :].astype(F32)).astype(BF16)
        ref[:, :width] = dot(whole, mine).astype(BF16)
        extra = dot(quarters[0], mine[:, :quarter])
        for i in range(1, 4):
            extra = extra + dot(quarters[i], mine[:, i * quarter : (i + 1) * quarter])
        ref[:, width:] = extra.astype(BF16)


def relay_kernel(near_ref, x_all_ref, out_ref):
    out_ref[...] = near_ref[:, near_ref.shape[1] - out_ref.shape[1] :]


def grad_kernel(inner_ref, full_ref, x_ref, out_ref):
    hid = full_ref.shape[2] - 128
    small = jnp.concatenate([full_ref[i, :, hid:].astype(F32) for i in range(N_CTX)], axis=0).astype(BF16)
    turned = to_rows(small)
    score = turned[0:1] + turned[1:2] + turned[2:3]
    inner = inner_ref[0]
    for i in range(1, N_CTX):
        inner = inner + inner_ref[i]
    slope = inner * (score * (1.0 - score))
    a, b, c = pieces(slope)
    line = iota(slope.shape, 0)
    slope = jnp.where(line == 0, a.astype(F32), jnp.where(line == 1, b.astype(F32), jnp.where(line == 2, c.astype(F32), 0.0)))
    grad = jnp.sum(dot(slope.astype(BF16), x_ref[...]), axis=0, keepdims=True)
    copies = out_ref.shape[0]
    lines = []
    for j in range(8):
        lines.append(grad[:, j * 128 : (j + 1) * 128])
    block = jnp.concatenate(lines, axis=0).astype(out_ref.dtype)
    for k in range(copies):
        out_ref[k] = block


def merge_kernel(near_ref, far_ref, grads_ref, out_ref):
    span = near_ref.shape[1]
    out_ref[:, :span] = near_ref[...]
    out_ref[:, span : 2 * span] = far_ref[...]
    parts = grads_ref.shape[0] // 2
    for zh in range(2):
        total = grads_ref[zh].astype(F32)
        for k in range(1, parts):
            total = total + grads_ref[2 * k + zh].astype(F32)
        high = total.astype(BF16)
        low = (total - high.astype(F32)).astype(BF16)
        for at, v in ((2 * span + zh * 128, high), (2 * span + 256 + zh * 128, low)):
            out_ref[:, at : at + 128] = jnp.concatenate([v.astype(F32)] * HALF, axis=0).astype(BF16)


def out_kernel(zh_ref, route_ref, fin_ref, out_ref, grad_ref):
    far, place, position = where_to(zh_ref[0], route_ref[...])
    count, width = out_ref.shape
    quarter = width // 4
    span = width + quarter
    n = HALF * BACK
    slots = iota((count, n), 1)
    base = place * BACK
    for half in range(2):
        here = far == half
        of_main = pick((slots == base + position) & (position < BACK) & here)
        main = dot(of_main, fin_ref[:, half * span : half * span + width])
        extra = fin_ref[:, half * span + width : (half + 1) * span]
        for i in range(4):
            cols = slice(i * quarter, (i + 1) * quarter)
            of_extra = pick((slots == base + (position - BACK) * 4 + i) & (position >= BACK) & here)
            value = main[:, cols] + dot(of_extra, extra)
            if half:
                value = value + out_ref[:, cols].astype(F32)
            out_ref[:, cols] = value.astype(BF16)
    line, r = iota((N_EXP, n), 0), iota((N_EXP, n), 1)
    place = jnp.where(line >= HALF, line - HALF, line)
    for j in range(8):
        total = jnp.zeros((N_EXP, 128), F32)
        for zh in range(2):
            take = pick((r == place * BACK + j) & ((line >= HALF) == (zh == 1)))
            for part in range(2):
                at = 2 * span + part * 256 + zh * 128
                total = total + dot(take, fin_ref[:, at : at + 128])
        grad_ref[:, j * 128 : (j + 1) * 128] = total


def call(kernel, out, scalars=0, scratch=()):
    def run(*args):
        smem = pl.BlockSpec(memory_space=pltpu.SMEM)
        vmem = pl.BlockSpec(memory_space=pltpu.VMEM)
        specs = [smem if i < scalars else vmem for i in range(len(args))]
        return pl.pallas_call(
            kernel,
            in_specs=specs,
            out_specs=jax.tree.map(lambda _: vmem, out),
            out_shape=out,
            scratch_shapes=scratch,
            compiler_params=pltpu.CompilerParams(vmem_limit_bytes=16 * 1024 * 1024),
        )(*args)

    return run


def as_one_step(turns, body, state):
    out = lax.while_loop(lambda s: s[0] < turns, lambda s: (s[0] + 1, *body(s[0], *s[1:])), (jnp.int32(0), *state))
    return out[1:]


def shards(tokens, routes, router_weight, gate_weight, up_weight, down_weight, cotangent):
    count, width = tokens.shape
    hid = gate_weight.shape[2]
    shape = jax.ShapeDtypeStruct
    zh = lax.axis_index("zh").astype(I32)
    expert = zh * HALF + lax.axis_index("y") * 2 + lax.axis_index("core")
    zh = zh.reshape(1)
    turns = 1 + lax.axis_index("ctx").astype(I32) // N_CTX
    span = width + width // 4
    rows = N_EXP * CAP
    exchange = functools.partial(lax.all_to_all, axis_name=IN_Z, split_axis=0, concat_axis=0, tiled=True)
    over_ctx = functools.partial(lax.all_to_all, axis_name="ctx", split_axis=0, concat_axis=0, tiled=True)

    chunk = shape((HALF * BACK, span), BF16)
    wide = shape((rows, width), BF16)
    x_far, near, x, full = call(
        pack_kernel,
        (chunk, shape((HALF * BACK, 3 * span), BF16), wide, shape((N_CTX, rows // N_CTX, hid + 128), BF16)),
        1,
    )(zh, routes, tokens, cotangent)
    x_far = lax.ppermute(x_far, PAIR, PAIR_PERM)
    (near,) = as_one_step(turns, lambda turn, v: (exchange(v),), (near,))
    x_all = exchange(x_far)
    cot_far = lax.ppermute(call(relay_kernel, chunk)(near, x_all), PAIR, PAIR_PERM)

    router_col = lax.dynamic_slice(router_weight, (lax.axis_index("ctx") * width, expert), (width, 1))
    router_col = jnp.concatenate([*pieces(router_col), jnp.zeros((width, 125), BF16)], axis=1)
    part = shape((N_CTX, rows // N_CTX, 2 * hid + 128), BF16)

    def to_hidden(turn, x, full):
        weights = router_col, gate_weight[0], up_weight[0]
        sums, x = call(up_kernel, (part, wide), 1)(turn.reshape(1), near, x_all, *weights)
        return x, over_ctx(call(hidden_kernel, shape(full.shape, BF16))(over_ctx(sums)))

    x, full = as_one_step(turns, to_hidden, (x, full))

    near_back, far, inner = call(
        down_kernel,
        (chunk, chunk, shape((N_CTX, 8, rows), F32)),
        scratch=[pltpu.VMEM((rows, width), BF16)],
    )(full, near, cot_far, down_weight[0])
    far = lax.ppermute(far, PAIR, PAIR_PERM)
    inner = over_ctx(inner)
    grad = call(grad_kernel, shape((lax.axis_size(ALL_Z), 8, width // 8), BF16))(inner, full, x)

    (grads,) = as_one_step(turns, lambda turn, v: (lax.all_to_all(v, ALL_Z, 0, 0, tiled=True),), (grad,))
    fin = exchange(call(merge_kernel, shape((HALF * BACK, 2 * span + 512), BF16))(near_back, far, grads))
    block_out, grad = call(out_kernel, (shape((count, width), BF16), shape((N_EXP, width), F32)), 1)(zh, routes, fin)
    return block_out, grad.T


def solution(mesh):
    fine = Mesh(mesh.devices.reshape(MESH), NAMES)
    ep = ("zh", "y", "core")
    return jax.shard_map(
        shards,
        mesh=fine,
        in_specs=(
            P(TOK, "ctx"),
            P(TOK, None),
            P(),
            P(ep, "ctx", None),
            P(ep, "ctx", None),
            P(ep, None, "ctx"),
            P(TOK, "ctx"),
        ),
        out_specs=(P(TOK, "ctx"), P("ctx", None)),
        check_vma=False,
    )
```

```python
import functools

import jax
import jax.numpy as jnp
from jax import lax
from jax.experimental import pallas as pl
from jax.experimental.pallas import tpu as pltpu
from jax.sharding import Mesh, PartitionSpec as P

BF16 = jnp.bfloat16
F32 = jnp.float32
I32 = jnp.int32
CAP = 10
N_EXP = 16
N_CTX = 4
HALF = 8
BACK = 8
MESH = (2, 8, 4, 2, 4, 2)
NAMES = ("dh", "dl", "ctx", "zh", "y", "core")
TOK = ("dh", "dl", "zh", "y", "core")
ALL_Z = ("dh", "dl", "zh")
IN_Z = ("y", "core")
PAIR = ("dh", "zh")
PAIR_PERM = ((0, 3), (3, 0), (1, 2), (2, 1))


def dot(a, b, dims=((1,), (0,))):
    return lax.dot_general(a, b, (dims, ((), ())), preferred_element_type=F32)


def iota(shape, dim):
    return lax.broadcasted_iota(I32, shape, dim)


def pick(mask):
    return mask.astype(F32).astype(BF16)


def pieces(v):
    a = v.astype(BF16)
    v = v - a.astype(F32)
    b = v.astype(BF16)
    c = (v - b.astype(F32)).astype(BF16)
    return a, b, c


def spread(lane, first, v):
    a, b, c = pieces(v)
    out = jnp.where(lane == first, a.astype(F32), 0.0)
    out = jnp.where(lane == first + 1, b.astype(F32), out)
    return jnp.where(lane == first + 2, c.astype(F32), out)


def gathered(lane, first, v):
    return jnp.sum(jnp.where((lane >= first) & (lane < first + 3), v, 0.0), axis=1, keepdims=True)


def tenth(r):
    out = jnp.zeros_like(r)
    for k in range(1, HALF):
        out = out + (r >= k * CAP).astype(I32)
    return out


def where_to(zh, route):
    count = route.shape[0]
    ids = iota((count, 128), 1)
    onehot = (route == ids).astype(F32)
    before = pick(iota((count, count), 1) < iota((count, count), 0))
    earlier = dot(before, onehot.astype(BF16))
    position = jnp.sum(earlier * onehot, axis=1, keepdims=True).astype(I32)
    far = jnp.where(route >= HALF, 1, 0)
    far = jnp.where(zh == 1, 1 - far, far)
    place = jnp.where(route >= HALF, route - HALF, route)
    return far, place, position


def packing(base, position, shape):
    slots = iota(shape, 1)
    whole = pick((slots == base + position) & (position < BACK))
    quarters = [pick((slots == base + (position - BACK) * 4 + i) & (position >= BACK)) for i in range(4)]
    return whole, quarters


def pack_kernel(zh_ref, route_ref, tok_ref, cot_ref, far_ref, near_ref, full_ref):
    full_ref[...] = jnp.zeros(full_ref.shape, BF16)
    far, place, position = where_to(zh_ref[0], route_ref[...])
    count, width = tok_ref.shape
    quarter = width // 4
    span = width + quarter
    n = HALF * BACK
    whole, quarters = packing(far * n + place * BACK, position, (count, 2 * n))
    turn = ((0,), (0,))
    for ref, near_at, far_out, far_at in ((tok_ref, 0, far_ref, 0), (cot_ref, span, near_ref, 2 * span)):
        main = dot(whole, ref[...], turn).astype(BF16)
        extra = dot(quarters[0], ref[:, :quarter], turn)
        for i in range(1, 4):
            extra = extra + dot(quarters[i], ref[:, i * quarter : (i + 1) * quarter], turn)
        extra = extra.astype(BF16)
        near_ref[:, near_at : near_at + width], near_ref[:, near_at + width : near_at + span] = main[:n], extra[:n]
        far_out[:, far_at : far_at + width], far_out[:, far_at + width : far_at + span] = main[n:], extra[n:]


def unpacking():
    shape = (HALF * CAP, HALF * BACK)
    r, col = iota(shape, 0), iota(shape, 1)
    src = tenth(r)
    p = r - src * CAP
    whole = pick((col == src * BACK + p) & (p < BACK))
    quarters = [pick((col == src * BACK + (p - BACK) * 4 + i) & (p >= BACK)) for i in range(4)]
    return whole, quarters


def unpack(maps, main, extra):
    whole, quarters = maps
    quarter = extra.shape[1]
    return [dot(whole, main[:, i * quarter : (i + 1) * quarter]) + dot(quarters[i], extra) for i in range(4)]


def up_kernel(near_ref, far_ref, router_ref, gate_ref, up_ref, part_ref, x_ref):
    width, hid = gate_ref.shape
    quarter = width // 4
    span = width + quarter
    n = HALF * CAP
    maps = unpacking()
    for half, ref in enumerate((near_ref, far_ref)):
        for i, block in enumerate(unpack(maps, ref[:, :width], ref[:, width:span])):
            x_ref[half * n : (half + 1) * n, i * quarter : (i + 1) * quarter] = block.astype(BF16)
    x = x_ref[...]
    rows = 2 * n // N_CTX

    def put(v, at):
        for i in range(N_CTX):
            part_ref[i, :, at : at + v.shape[1]] = v[i * rows : (i + 1) * rows].astype(BF16)

    logit = jnp.sum(dot(x, router_ref[...]), axis=1, keepdims=True)
    put(spread(iota((2 * n, 128), 1), 0, logit), 2 * hid)
    put(dot(x, gate_ref[...]), 0)
    put(dot(x, up_ref[...]), hid)


def hidden_kernel(turn_ref, mine_ref, out_ref):
    hid = (mine_ref.shape[2] - 128) // 2

    def total(at, size):
        out = mine_ref[0, :, at : at + size].astype(F32)
        for i in range(1, N_CTX):
            out = out + mine_ref[i, :, at : at + size].astype(F32)
        return out

    gate, up = total(0, hid), total(hid, hid)
    logit = jnp.sum(total(2 * hid, 128), axis=1, keepdims=True)
    hidden = (gate / (1.0 + jnp.exp(-gate)) * up).astype(BF16)
    score = 1.0 / (1.0 + jnp.exp(-logit))
    small = spread(iota((hidden.shape[0], 128), 1), 0, score).astype(BF16)
    for i in range(N_CTX):
        out_ref[i, :, :hid] = hidden
        out_ref[i, :, hid:] = small


def to_rows(v):
    size = v.shape[0]
    eye = pick(iota((size, size), 0) == iota((size, size), 1))
    return dot(v, eye, ((0,), (0,)))


def down_kernel(full_ref, down_ref, near_ref, far_ref, values_ref):
    hid, width = down_ref.shape
    quarter = width // 4
    full = jnp.concatenate([full_ref[i].astype(F32) for i in range(N_CTX)], axis=0)
    score = gathered(iota((full.shape[0], 128), 1), 0, full[:, hid:])
    values_ref[...] = dot(full[:, :hid].astype(BF16), down_ref[...]).astype(BF16)
    n = HALF * CAP
    slot, r = iota((HALF * BACK, n), 0), iota((HALF * BACK, n), 1)
    src = tenth(r)
    p = r - src * CAP
    whole = pick((slot == src * BACK + p) & (p < BACK))
    quarters = [pick((slot == src * BACK + (p - BACK) * 4 + i) & (p >= BACK)) for i in range(4)]
    for half, ref in enumerate((near_ref, far_ref)):
        part = slice(half * n, (half + 1) * n)
        mine = (score[part] * values_ref[part, :].astype(F32)).astype(BF16)
        ref[:, :width] = dot(whole, mine).astype(BF16)
        extra = dot(quarters[0], mine[:, :quarter])
        for i in range(1, 4):
            extra = extra + dot(quarters[i], mine[:, i * quarter : (i + 1) * quarter])
        ref[:, width:] = extra.astype(BF16)


def inner_kernel(near_ref, far_ref, values_ref, inner_ref):
    rows, width = values_ref.shape
    quarter = width // 4
    span = width + quarter
    n = HALF * CAP
    maps = unpacking()
    sums = []
    for half, (ref, at) in enumerate(((near_ref, span), (far_ref, 0))):
        inner = jnp.zeros((n, 1), F32)
        for i, block in enumerate(unpack(maps, ref[:, at : at + width], ref[:, at + width : at + span])):
            value = values_ref[half * n : (half + 1) * n, i * quarter : (i + 1) * quarter].astype(F32)
            inner = inner + jnp.sum(block * value, axis=1, keepdims=True)
        sums.append(inner)
    turned = to_rows(spread(iota((rows, 128), 1), 0, jnp.concatenate(sums, axis=0)).astype(BF16))
    inner = turned[0:1] + turned[1:2] + turned[2:3]
    for i in range(N_CTX):
        inner_ref[i] = jnp.broadcast_to(inner, inner_ref.shape[1:])


def relay_kernel(near_ref, sums_ref, out_ref):
    out_ref[...] = near_ref[:, near_ref.shape[1] - out_ref.shape[1] :]


def grad_kernel(inner_ref, full_ref, x_ref, out_ref):
    hid = full_ref.shape[2] - 128
    small = jnp.concatenate([full_ref[i, :, hid:].astype(F32) for i in range(N_CTX)], axis=0).astype(BF16)
    turned = to_rows(small)
    score = turned[0:1] + turned[1:2] + turned[2:3]
    inner = inner_ref[0]
    for i in range(1, N_CTX):
        inner = inner + inner_ref[i]
    slope = inner * (score * (1.0 - score))
    a, b, c = pieces(slope)
    line = iota(slope.shape, 0)
    slope = jnp.where(line == 0, a.astype(F32), jnp.where(line == 1, b.astype(F32), jnp.where(line == 2, c.astype(F32), 0.0)))
    grad = jnp.sum(dot(slope.astype(BF16), x_ref[...]), axis=0, keepdims=True)
    copies = out_ref.shape[0]
    lines = []
    for j in range(8):
        lines.append(grad[:, j * 128 : (j + 1) * 128])
    block = jnp.concatenate(lines, axis=0).astype(out_ref.dtype)
    for k in range(copies):
        out_ref[k] = block


def merge_kernel(near_ref, far_ref, grads_ref, out_ref):
    span = near_ref.shape[1]
    out_ref[:, :span] = near_ref[...]
    out_ref[:, span : 2 * span] = far_ref[...]
    parts = grads_ref.shape[0] // 2
    for zh in range(2):
        total = grads_ref[zh].astype(F32)
        for k in range(1, parts):
            total = total + grads_ref[2 * k + zh].astype(F32)
        high = total.astype(BF16)
        low = (total - high.astype(F32)).astype(BF16)
        for at, v in ((2 * span + zh * 128, high), (2 * span + 256 + zh * 128, low)):
            out_ref[:, at : at + 128] = jnp.concatenate([v.astype(F32)] * HALF, axis=0).astype(BF16)


def out_kernel(zh_ref, route_ref, fin_ref, out_ref, grad_ref):
    far, place, position = where_to(zh_ref[0], route_ref[...])
    count, width = out_ref.shape
    quarter = width // 4
    span = width + quarter
    n = HALF * BACK
    slots = iota((count, n), 1)
    base = place * BACK
    for half in range(2):
        here = far == half
        of_main = pick((slots == base + position) & (position < BACK) & here)
        main = dot(of_main, fin_ref[:, half * span : half * span + width])
        extra = fin_ref[:, half * span + width : (half + 1) * span]
        for i in range(4):
            cols = slice(i * quarter, (i + 1) * quarter)
            of_extra = pick((slots == base + (position - BACK) * 4 + i) & (position >= BACK) & here)
            value = main[:, cols] + dot(of_extra, extra)
            if half:
                value = value + out_ref[:, cols].astype(F32)
            out_ref[:, cols] = value.astype(BF16)
    line, r = iota((N_EXP, n), 0), iota((N_EXP, n), 1)
    place = jnp.where(line >= HALF, line - HALF, line)
    for j in range(8):
        total = jnp.zeros((N_EXP, 128), F32)
        for zh in range(2):
            take = pick((r == place * BACK + j) & ((line >= HALF) == (zh == 1)))
            for part in range(2):
                at = 2 * span + part * 256 + zh * 128
                total = total + dot(take, fin_ref[:, at : at + 128])
        grad_ref[:, j * 128 : (j + 1) * 128] = total


def call(kernel, out, scalars=0, scratch=()):
    def run(*args):
        smem = pl.BlockSpec(memory_space=pltpu.SMEM)
        vmem = pl.BlockSpec(memory_space=pltpu.VMEM)
        specs = [smem if i < scalars else vmem for i in range(len(args))]
        return pl.pallas_call(
            kernel,
            in_specs=specs,
            out_specs=jax.tree.map(lambda _: vmem, out),
            out_shape=out,
            scratch_shapes=scratch,
            compiler_params=pltpu.CompilerParams(vmem_limit_bytes=16 * 1024 * 1024),
        )(*args)

    return run


def as_one_step(turns, body, state):
    out = lax.while_loop(lambda s: s[0] < turns, lambda s: (s[0] + 1, *body(s[0], *s[1:])), (jnp.int32(0), *state))
    return out[1:]


def shards(tokens, routes, router_weight, gate_weight, up_weight, down_weight, cotangent):
    count, width = tokens.shape
    hid = gate_weight.shape[2]
    shape = jax.ShapeDtypeStruct
    zh = lax.axis_index("zh").astype(I32)
    expert = zh * HALF + lax.axis_index("y") * 2 + lax.axis_index("core")
    zh = zh.reshape(1)
    turns = 1 + lax.axis_index("ctx").astype(I32) // N_CTX
    span = width + width // 4
    rows = N_EXP * CAP
    exchange = functools.partial(lax.all_to_all, axis_name=IN_Z, split_axis=0, concat_axis=0, tiled=True)
    over_ctx = functools.partial(lax.all_to_all, axis_name="ctx", split_axis=0, concat_axis=0, tiled=True)

    chunk = shape((HALF * BACK, span), BF16)
    wide = shape((rows, width), BF16)
    x_far, near, full = call(
        pack_kernel,
        (chunk, shape((HALF * BACK, 3 * span), BF16), shape((N_CTX, rows // N_CTX, hid + 128), BF16)),
        1,
    )(zh, routes, tokens, cotangent)
    x_far = lax.ppermute(x_far, PAIR, PAIR_PERM)
    (near,) = as_one_step(turns, lambda turn, v: (exchange(v),), (near,))
    x_all = exchange(x_far)

    router_col = lax.dynamic_slice(router_weight, (lax.axis_index("ctx") * width, expert), (width, 1))
    router_col = jnp.concatenate([*pieces(router_col), jnp.zeros((width, 125), BF16)], axis=1)
    part = shape((N_CTX, rows // N_CTX, 2 * hid + 128), BF16)
    sums, x = call(up_kernel, (part, wide))(near, x_all, router_col, gate_weight[0], up_weight[0])
    cot_far = lax.ppermute(call(relay_kernel, chunk)(near, sums), PAIR, PAIR_PERM)
    mine = over_ctx(sums)

    def to_hidden(turn, full):
        return (over_ctx(call(hidden_kernel, shape(full.shape, BF16), 1)(turn.reshape(1), mine)),)

    (full,) = as_one_step(turns, to_hidden, (full,))

    near_back, far, values = call(down_kernel, (chunk, chunk, wide))(full, down_weight[0])
    far = lax.ppermute(far, PAIR, PAIR_PERM)
    inner = over_ctx(call(inner_kernel, shape((N_CTX, 8, rows), F32))(near, cot_far, values))
    grad = call(grad_kernel, shape((lax.axis_size(ALL_Z), 8, width // 8), BF16))(inner, full, x)

    (grads,) = as_one_step(turns, lambda turn, v: (lax.all_to_all(v, ALL_Z, 0, 0, tiled=True),), (grad,))
    fin = exchange(call(merge_kernel, shape((HALF * BACK, 2 * span + 512), BF16))(near_back, far, grads))
    block_out, grad = call(out_kernel, (shape((count, width), BF16), shape((N_EXP, width), F32)), 1)(zh, routes, fin)
    return block_out, grad.T


def solution(mesh):
    fine = Mesh(mesh.devices.reshape(MESH), NAMES)
    ep = ("zh", "y", "core")
    return jax.shard_map(
        shards,
        mesh=fine,
        in_specs=(
            P(TOK, "ctx"),
            P(TOK, None),
            P(),
            P(ep, "ctx", None),
            P(ep, "ctx", None),
            P(ep, None, "ctx"),
            P(TOK, "ctx"),
        ),
        out_specs=(P(TOK, "ctx"), P("ctx", None)),
        check_vma=False,
    )
```

```python
import functools

import jax
import jax.numpy as jnp
from jax import lax
from jax.experimental import pallas as pl
from jax.experimental.pallas import tpu as pltpu
from jax.sharding import Mesh, PartitionSpec as P

BF16 = jnp.bfloat16
F32 = jnp.float32
I32 = jnp.int32
CAP = 10
N_EXP = 16
N_CTX = 4
HALF = 8
BACK = 8
MESH = (2, 8, 4, 2, 4, 2)
NAMES = ("dh", "dl", "ctx", "zh", "y", "core")
TOK = ("dh", "dl", "zh", "y", "core")
ALL_Z = ("dh", "dl", "zh")
IN_Z = ("y", "core")
PAIR = ("dh", "zh")
PAIR_PERM = ((0, 3), (3, 0), (1, 2), (2, 1))


def dot(a, b, dims=((1,), (0,))):
    return lax.dot_general(a, b, (dims, ((), ())), preferred_element_type=F32)


def iota(shape, dim):
    return lax.broadcasted_iota(I32, shape, dim)


def pick(mask):
    return mask.astype(F32).astype(BF16)


def pieces(v):
    a = v.astype(BF16)
    v = v - a.astype(F32)
    b = v.astype(BF16)
    c = (v - b.astype(F32)).astype(BF16)
    return a, b, c


def spread(lane, first, v):
    a, b, c = pieces(v)
    out = jnp.where(lane == first, a.astype(F32), 0.0)
    out = jnp.where(lane == first + 1, b.astype(F32), out)
    return jnp.where(lane == first + 2, c.astype(F32), out)


def gathered(lane, first, v):
    return jnp.sum(jnp.where((lane >= first) & (lane < first + 3), v, 0.0), axis=1, keepdims=True)


def tenth(r):
    out = jnp.zeros_like(r)
    for k in range(1, HALF):
        out = out + (r >= k * CAP).astype(I32)
    return out


def where_to(zh, routes):
    count = routes.shape[1]
    own = iota((count, count), 0) == iota((count, count), 1)
    route = jnp.sum(jnp.where(own, routes, 0).astype(F32), axis=1, keepdims=True).astype(I32)
    ids = iota((count, 128), 1)
    onehot = (route == ids).astype(F32)
    before = pick(iota((count, count), 1) < iota((count, count), 0))
    earlier = dot(before, onehot.astype(BF16))
    position = jnp.sum(earlier * onehot, axis=1, keepdims=True).astype(I32)
    far = jnp.where(route >= HALF, 1, 0)
    far = jnp.where(zh == 1, 1 - far, far)
    place = jnp.where(route >= HALF, route - HALF, route)
    return far, place, position


def packing(base, position, shape):
    slots = iota(shape, 1)
    whole = pick((slots == base + position) & (position < BACK))
    quarters = [pick((slots == base + (position - BACK) * 4 + i) & (position >= BACK)) for i in range(4)]
    return whole, quarters


def pack_kernel(zh_ref, routes_ref, tok_ref, cot_ref, far_ref, near_ref, x_ref, full_ref):
    x_ref[...] = jnp.zeros(x_ref.shape, BF16)
    full_ref[...] = jnp.zeros(full_ref.shape, BF16)
    far, place, position = where_to(zh_ref[0], routes_ref[...])
    count, width = tok_ref.shape
    quarter = width // 4
    span = width + quarter
    n = HALF * BACK
    whole, quarters = packing(far * n + place * BACK, position, (count, 2 * n))
    turn = ((0,), (0,))
    for ref, near_at, far_out, far_at in ((tok_ref, 0, far_ref, 0), (cot_ref, span, near_ref, 2 * span)):
        main = dot(whole, ref[...], turn).astype(BF16)
        extra = dot(quarters[0], ref[:, :quarter], turn)
        for i in range(1, 4):
            extra = extra + dot(quarters[i], ref[:, i * quarter : (i + 1) * quarter], turn)
        extra = extra.astype(BF16)
        near_ref[:, near_at : near_at + width], near_ref[:, near_at + width : near_at + span] = main[:n], extra[:n]
        far_out[:, far_at : far_at + width], far_out[:, far_at + width : far_at + span] = main[n:], extra[n:]


def unpacking():
    shape = (HALF * CAP, HALF * BACK)
    r, col = iota(shape, 0), iota(shape, 1)
    src = tenth(r)
    p = r - src * CAP
    whole = pick((col == src * BACK + p) & (p < BACK))
    quarters = [pick((col == src * BACK + (p - BACK) * 4 + i) & (p >= BACK)) for i in range(4)]
    return whole, quarters


def unpack(maps, main, extra):
    whole, quarters = maps
    quarter = extra.shape[1]
    return [dot(whole, main[:, i * quarter : (i + 1) * quarter]) + dot(quarters[i], extra) for i in range(4)]


def up_kernel(turn_ref, near_ref, far_ref, router_ref, gate_in, up_in, part_ref, x_ref, gate_ref, up_ref, sems):
    moves = [pltpu.make_async_copy(gate_in.at[0], gate_ref, sems.at[0]), pltpu.make_async_copy(up_in.at[0], up_ref, sems.at[1])]
    for move in moves:
        move.start()
    width, hid = gate_ref.shape
    quarter = width // 4
    span = width + quarter
    n = HALF * CAP
    maps = unpacking()
    for half, ref in enumerate((near_ref, far_ref)):
        for i, block in enumerate(unpack(maps, ref[:, :width], ref[:, width:span])):
            x_ref[half * n : (half + 1) * n, i * quarter : (i + 1) * quarter] = block.astype(BF16)
    x = x_ref[...]
    rows = 2 * n // N_CTX

    def put(v, at):
        for i in range(N_CTX):
            part_ref[i, :, at : at + v.shape[1]] = v[i * rows : (i + 1) * rows].astype(BF16)

    logit = jnp.sum(dot(x, router_ref[...]), axis=1, keepdims=True)
    put(spread(iota((2 * n, 128), 1), 0, logit), 2 * hid)
    moves[0].wait()
    put(dot(x, gate_ref[...]), 0)
    moves[1].wait()
    put(dot(x, up_ref[...]), hid)


def hidden_kernel(mine_ref, out_ref):
    hid = (mine_ref.shape[2] - 128) // 2

    def total(at, size):
        out = mine_ref[0, :, at : at + size].astype(F32)
        for i in range(1, N_CTX):
            out = out + mine_ref[i, :, at : at + size].astype(F32)
        return out

    gate, up = total(0, hid), total(hid, hid)
    logit = jnp.sum(total(2 * hid, 128), axis=1, keepdims=True)
    hidden = (gate / (1.0 + jnp.exp(-gate)) * up).astype(BF16)
    score = 1.0 / (1.0 + jnp.exp(-logit))
    small = spread(iota((hidden.shape[0], 128), 1), 0, score).astype(BF16)
    for i in range(N_CTX):
        out_ref[i, :, :hid] = hidden
        out_ref[i, :, hid:] = small


def to_rows(v):
    size = v.shape[0]
    eye = pick(iota((size, size), 0) == iota((size, size), 1))
    return dot(v, eye, ((0,), (0,)))


def down_kernel(full_ref, cot_near_ref, cot_far_ref, down_ref, near_ref, far_ref, inner_ref, values_ref):
    hid, width = down_ref.shape
    quarter = width // 4
    span = width + quarter
    full = jnp.concatenate([full_ref[i].astype(F32) for i in range(N_CTX)], axis=0)
    rows = full.shape[0]
    lane = iota((rows, 128), 1)
    score = gathered(lane, 0, full[:, hid:])
    values_ref[...] = dot(full[:, :hid].astype(BF16), down_ref[...]).astype(BF16)
    n = HALF * CAP
    maps = unpacking()
    sums = []
    for half, (ref, at) in enumerate(((cot_near_ref, span), (cot_far_ref, 0))):
        inner = jnp.zeros((n, 1), F32)
        for i, block in enumerate(unpack(maps, ref[:, at : at + width], ref[:, at + width : at + span])):
            value = values_ref[half * n : (half + 1) * n, i * quarter : (i + 1) * quarter].astype(F32)
            inner = inner + jnp.sum(block * value, axis=1, keepdims=True)
        sums.append(inner)
    turned = to_rows(spread(lane, 0, jnp.concatenate(sums, axis=0)).astype(BF16))
    inner = turned[0:1] + turned[1:2] + turned[2:3]
    for i in range(N_CTX):
        inner_ref[i] = jnp.broadcast_to(inner, inner_ref.shape[1:])
    slot, r = iota((HALF * BACK, n), 0), iota((HALF * BACK, n), 1)
    src = tenth(r)
    p = r - src * CAP
    whole = pick((slot == src * BACK + p) & (p < BACK))
    quarters = [pick((slot == src * BACK + (p - BACK) * 4 + i) & (p >= BACK)) for i in range(4)]
    for half, ref in enumerate((near_ref, far_ref)):
        part = slice(half * n, (half + 1) * n)
        mine = (score[part] * values_ref[part, :].astype(F32)).astype(BF16)
        ref[:, :width] = dot(whole, mine).astype(BF16)
        extra = dot(quarters[0], mine[:, :quarter])
        for i in range(1, 4):
            extra = extra + dot(quarters[i], mine[:, i * quarter : (i + 1) * quarter])
        ref[:, width:] = extra.astype(BF16)


def slice_kernel(near_ref, out_ref):
    out_ref[...] = near_ref[:, near_ref.shape[1] - out_ref.shape[1] :]


def gate_kernel(v_ref, other_ref, out_ref):
    pass


def grad_kernel(inner_ref, full_ref, x_ref, out_ref):
    hid = full_ref.shape[2] - 128
    small = jnp.concatenate([full_ref[i, :, hid:].astype(F32) for i in range(N_CTX)], axis=0).astype(BF16)
    turned = to_rows(small)
    score = turned[0:1] + turned[1:2] + turned[2:3]
    inner = inner_ref[0]
    for i in range(1, N_CTX):
        inner = inner + inner_ref[i]
    slope = inner * (score * (1.0 - score))
    a, b, c = pieces(slope)
    line = iota(slope.shape, 0)
    slope = jnp.where(line == 0, a.astype(F32), jnp.where(line == 1, b.astype(F32), jnp.where(line == 2, c.astype(F32), 0.0)))
    grad = jnp.sum(dot(slope.astype(BF16), x_ref[...]), axis=0, keepdims=True)
    copies = out_ref.shape[0]
    lines = []
    for j in range(8):
        lines.append(grad[:, j * 128 : (j + 1) * 128])
    block = jnp.concatenate(lines, axis=0).astype(out_ref.dtype)
    for k in range(copies):
        out_ref[k] = block


def merge_kernel(near_ref, far_ref, grads_ref, out_ref):
    span = near_ref.shape[1]
    out_ref[:, :span] = near_ref[...]
    out_ref[:, span : 2 * span] = far_ref[...]
    parts = grads_ref.shape[0] // 2
    for zh in range(2):
        total = grads_ref[zh].astype(F32)
        for k in range(1, parts):
            total = total + grads_ref[2 * k + zh].astype(F32)
        high = total.astype(BF16)
        low = (total - high.astype(F32)).astype(BF16)
        for at, v in ((2 * span + zh * 128, high), (2 * span + 256 + zh * 128, low)):
            out_ref[:, at : at + 128] = jnp.concatenate([v.astype(F32)] * HALF, axis=0).astype(BF16)


def out_kernel(zh_ref, routes_ref, fin_ref, out_ref, grad_ref):
    far, place, position = where_to(zh_ref[0], routes_ref[...])
    count, width = out_ref.shape
    quarter = width // 4
    span = width + quarter
    n = HALF * BACK
    slots = iota((count, n), 1)
    base = place * BACK
    for half in range(2):
        here = far == half
        of_main = pick((slots == base + position) & (position < BACK) & here)
        main = dot(of_main, fin_ref[:, half * span : half * span + width])
        extra = fin_ref[:, half * span + width : (half + 1) * span]
        for i in range(4):
            cols = slice(i * quarter, (i + 1) * quarter)
            of_extra = pick((slots == base + (position - BACK) * 4 + i) & (position >= BACK) & here)
            value = main[:, cols] + dot(of_extra, extra)
            if half:
                value = value + out_ref[:, cols].astype(F32)
            out_ref[:, cols] = value.astype(BF16)
    line, r = iota((N_EXP, n), 0), iota((N_EXP, n), 1)
    place = jnp.where(line >= HALF, line - HALF, line)
    for j in range(8):
        total = jnp.zeros((N_EXP, 128), F32)
        for zh in range(2):
            take = pick((r == place * BACK + j) & ((line >= HALF) == (zh == 1)))
            for part in range(2):
                at = 2 * span + part * 256 + zh * 128
                total = total + dot(take, fin_ref[:, at : at + 128])
        grad_ref[:, j * 128 : (j + 1) * 128] = total


def call(kernel, out, scalars=0, scratch=(), far_in=(), aliases={}):
    def run(*args):
        smem = pl.BlockSpec(memory_space=pltpu.SMEM)
        vmem = pl.BlockSpec(memory_space=pltpu.VMEM)
        anywhere = pl.BlockSpec(memory_space=pl.ANY)
        specs = [smem if i < scalars else anywhere if i in far_in else vmem for i in range(len(args))]
        return pl.pallas_call(
            kernel,
            in_specs=specs,
            out_specs=jax.tree.map(lambda _: vmem, out),
            out_shape=out,
            scratch_shapes=scratch,
            input_output_aliases=aliases,
            compiler_params=pltpu.CompilerParams(vmem_limit_bytes=16 * 1024 * 1024),
        )(*args)

    return run


def as_one_step(turns, body, state):
    out = lax.while_loop(lambda s: s[0] < turns, lambda s: (s[0] + 1, *body(s[0], *s[1:])), (jnp.int32(0), *state))
    return out[1:]


def shards(tokens, routes, router_weight, gate_weight, up_weight, down_weight, cotangent):
    count, width = tokens.shape
    routes = routes.reshape(1, count)
    hid = gate_weight.shape[2]
    shape = jax.ShapeDtypeStruct
    zh = lax.axis_index("zh").astype(I32)
    expert = zh * HALF + lax.axis_index("y") * 2 + lax.axis_index("core")
    zh = zh.reshape(1)
    turns = 1 + lax.axis_index("ctx").astype(I32) // N_CTX
    span = width + width // 4
    rows = N_EXP * CAP
    exchange = functools.partial(lax.all_to_all, axis_name=IN_Z, split_axis=0, concat_axis=0, tiled=True)
    over_ctx = functools.partial(lax.all_to_all, axis_name="ctx", split_axis=0, concat_axis=0, tiled=True)

    chunk = shape((HALF * BACK, span), BF16)
    wide = shape((rows, width), BF16)
    x_far, near, x, full = call(
        pack_kernel,
        (chunk, shape((HALF * BACK, 3 * span), BF16), wide, shape((N_CTX, rows // N_CTX, hid + 128), BF16)),
        1,
    )(zh, routes, tokens, cotangent)
    x_far = lax.ppermute(x_far, PAIR, PAIR_PERM)
    (near,) = as_one_step(turns, lambda turn, v: (exchange(v),), (near,))
    x_all = exchange(x_far)
    cot_far = call(gate_kernel, chunk, aliases={0: 0})(call(slice_kernel, chunk)(near), x_all)
    cot_far = lax.ppermute(cot_far, PAIR, PAIR_PERM)

    router_col = lax.dynamic_slice(router_weight, (lax.axis_index("ctx") * width, expert), (width, 1))
    router_col = jnp.concatenate([*pieces(router_col), jnp.zeros((width, 125), BF16)], axis=1)
    part = shape((N_CTX, rows // N_CTX, 2 * hid + 128), BF16)

    loads = [pltpu.VMEM((width, hid), BF16), pltpu.VMEM((width, hid), BF16), pltpu.SemaphoreType.DMA((2,))]

    def to_hidden(turn, x, full):
        weights = router_col, gate_weight, up_weight
        sums, x = call(up_kernel, (part, wide), 1, loads, (4, 5))(turn.reshape(1), near, x_all, *weights)
        return x, over_ctx(call(hidden_kernel, shape(full.shape, BF16))(over_ctx(sums)))

    x, full = as_one_step(turns, to_hidden, (x, full))

    near_back, far, inner = call(
        down_kernel,
        (chunk, chunk, shape((N_CTX, 8, rows), F32)),
        scratch=[pltpu.VMEM((rows, width), BF16)],
    )(full, near, cot_far, down_weight[0])
    far = lax.ppermute(far, PAIR, PAIR_PERM)
    inner = over_ctx(inner)
    grad = call(grad_kernel, shape((lax.axis_size(ALL_Z), 8, width // 8), BF16))(inner, full, x)

    (grads,) = as_one_step(turns, lambda turn, v: (lax.all_to_all(v, ALL_Z, 0, 0, tiled=True),), (grad,))
    fin = exchange(call(merge_kernel, shape((HALF * BACK, 2 * span + 512), BF16))(near_back, far, grads))
    block_out, grad = call(out_kernel, (shape((count, width), BF16), shape((N_EXP, width), F32)), 1)(zh, routes, fin)
    return block_out, grad.T


def solution(mesh):
    fine = Mesh(mesh.devices.reshape(MESH), NAMES)
    ep = ("zh", "y", "core")
    return jax.shard_map(
        shards,
        mesh=fine,
        in_specs=(
            P(TOK, "ctx"),
            P(TOK, None),
            P(),
            P(ep, "ctx", None),
            P(ep, "ctx", None),
            P(ep, None, "ctx"),
            P(TOK, "ctx"),
        ),
        out_specs=(P(TOK, "ctx"), P("ctx", None)),
        check_vma=False,
    )
```

```python
import functools

import jax
import jax.numpy as jnp
from jax import lax
from jax.experimental import pallas as pl
from jax.experimental.pallas import tpu as pltpu
from jax.sharding import Mesh, PartitionSpec as P

BF16 = jnp.bfloat16
F32 = jnp.float32
I32 = jnp.int32
CAP = 10
N_EXP = 16
N_CTX = 4
BLOCK = 24
HALF = 8
BACK = 8
MESH = (2, 8, 4, 2, 4, 2)
NAMES = ("dh", "dl", "ctx", "zh", "y", "core")
TOK = ("dh", "dl", "zh", "y", "core")
ALL_Z = ("dh", "dl", "zh")
IN_Z = ("y", "core")
PAIR = ("dh", "zh")
PAIR_PERM = ((0, 3), (3, 0), (1, 2), (2, 1))


def dot(a, b, dims=((1,), (0,))):
    return lax.dot_general(a, b, (dims, ((), ())), preferred_element_type=F32)


def iota(shape, dim):
    return lax.broadcasted_iota(I32, shape, dim)


def pick(mask):
    return mask.astype(F32).astype(BF16)


def pieces(v):
    a = v.astype(BF16)
    v = v - a.astype(F32)
    b = v.astype(BF16)
    c = (v - b.astype(F32)).astype(BF16)
    return a, b, c


def spread(lane, first, v):
    a, b, c = pieces(v)
    out = jnp.where(lane == first, a.astype(F32), 0.0)
    out = jnp.where(lane == first + 1, b.astype(F32), out)
    return jnp.where(lane == first + 2, c.astype(F32), out)


def gathered(lane, first, v):
    return jnp.sum(jnp.where((lane >= first) & (lane < first + 3), v, 0.0), axis=1, keepdims=True)


def places(q):
    block = jnp.zeros_like(q)
    for k in range(1, N_CTX):
        block = block + (q >= k * BLOCK).astype(I32)
    k = q - block * BLOCK
    second = (k >= CAP).astype(I32)
    return block * 2 + second, k - second * CAP, k < 2 * CAP


def where_to(zh, routes):
    count = routes.shape[1]
    own = iota((count, count), 0) == iota((count, count), 1)
    route = jnp.sum(jnp.where(own, routes, 0).astype(F32), axis=1, keepdims=True).astype(I32)
    ids = iota((count, 128), 1)
    onehot = (route == ids).astype(F32)
    before = pick(iota((count, count), 1) < iota((count, count), 0))
    earlier = dot(before, onehot.astype(BF16))
    position = jnp.sum(earlier * onehot, axis=1, keepdims=True).astype(I32)
    far = jnp.where(route >= HALF, 1, 0)
    far = jnp.where(zh == 1, 1 - far, far)
    place = jnp.where(route >= HALF, route - HALF, route)
    return far, place, position


def packing(base, position, shape):
    slots = iota(shape, 1)
    whole = pick((slots == base + position) & (position < BACK))
    quarters = [pick((slots == base + (position - BACK) * 4 + i) & (position >= BACK)) for i in range(4)]
    return whole, quarters


def pack_kernel(zh_ref, routes_ref, tok_ref, cot_ref, far_ref, near_ref, x_ref, mine_ref, full_ref):
    for ref in (x_ref, mine_ref, full_ref):
        ref[...] = jnp.zeros(ref.shape, BF16)
    far, place, position = where_to(zh_ref[0], routes_ref[...])
    count, width = tok_ref.shape
    quarter = width // 4
    span = width + quarter
    n = HALF * BACK
    whole, quarters = packing(far * n + place * BACK, position, (count, 2 * n))
    turn = ((0,), (0,))
    for ref, near_at, far_out, far_at in ((tok_ref, 0, far_ref, 0), (cot_ref, span, near_ref, 2 * span)):
        main = dot(whole, ref[...], turn).astype(BF16)
        extra = dot(quarters[0], ref[:, :quarter], turn)
        for i in range(1, 4):
            extra = extra + dot(quarters[i], ref[:, i * quarter : (i + 1) * quarter], turn)
        extra = extra.astype(BF16)
        near_ref[:, near_at : near_at + width], near_ref[:, near_at + width : near_at + span] = main[:n], extra[:n]
        far_out[:, far_at : far_at + width], far_out[:, far_at + width : far_at + span] = main[n:], extra[n:]


def chunk_maps(q, slot):
    src, p, real = places(q)
    whole = pick((slot == src * BACK + p) & (p < BACK) & real)
    quarters = [pick((slot == src * BACK + (p - BACK) * 4 + i) & (p >= BACK) & real) for i in range(4)]
    return whole, quarters


def unpacking():
    shape = (N_CTX * BLOCK, HALF * BACK)
    return chunk_maps(iota(shape, 0), iota(shape, 1))


def unpack(maps, main, extra):
    whole, quarters = maps
    quarter = extra.shape[1]
    return [dot(whole, main[:, i * quarter : (i + 1) * quarter]) + dot(quarters[i], extra) for i in range(4)]


def up_kernel(turn_ref, rows_ref, router_ref, gate_ref, up_ref, part_ref, x_ref):
    width, hid = gate_ref.shape
    quarter = width // 4
    for i, block in enumerate(unpack(unpacking(), rows_ref[:, :width], rows_ref[:, width : width + quarter])):
        x_ref[:, i * quarter : (i + 1) * quarter] = block.astype(BF16)
    x = x_ref[...]

    def put(v, at):
        for i in range(N_CTX):
            part_ref[i, :, at : at + v.shape[1]] = v[i * BLOCK : (i + 1) * BLOCK].astype(BF16)

    logit = jnp.sum(dot(x, router_ref[...]), axis=1, keepdims=True)
    put(spread(iota((N_CTX * BLOCK, 128), 1), 0, logit), 2 * hid)
    put(dot(x, gate_ref[...]), 0)
    put(dot(x, up_ref[...]), hid)


def hidden_kernel(near_ref, far_ref, out_ref):
    hid = (near_ref.shape[2] - 128) // 2
    halves = []
    for ref in (near_ref, far_ref):

        def total(at, size):
            out = ref[0, :, at : at + size].astype(F32)
            for i in range(1, N_CTX):
                out = out + ref[i, :, at : at + size].astype(F32)
            return out

        gate, up = total(0, hid), total(hid, hid)
        logit = jnp.sum(total(2 * hid, 128), axis=1, keepdims=True)
        score = 1.0 / (1.0 + jnp.exp(-logit))
        halves.append((gate / (1.0 + jnp.exp(-gate)) * up, spread(iota((BLOCK, 128), 1), 0, score)))
    hidden, small = (jnp.concatenate(v, axis=0).astype(BF16) for v in zip(*halves))
    for i in range(N_CTX):
        out_ref[i, :, :hid] = hidden
        out_ref[i, :, hid:] = small


def half_of(v, half):
    at = [(2 * i + half) * BLOCK for i in range(N_CTX)]
    return jnp.concatenate([v[k : k + BLOCK] for k in at], axis=0)


def to_rows(v):
    size = v.shape[0]
    eye = pick(iota((size, size), 0) == iota((size, size), 1))
    return dot(v, eye, ((0,), (0,)))


def down_kernel(full_ref, cot_near_ref, cot_far_ref, down_ref, near_ref, far_ref, inner_ref):
    hid, width = down_ref.shape
    quarter = width // 4
    span = width + quarter
    full = jnp.concatenate([full_ref[i].astype(F32) for i in range(N_CTX)], axis=0)
    score = gathered(iota((full.shape[0], 128), 1), 0, full[:, hid:])
    values = dot(full[:, :hid].astype(BF16), down_ref[...]).astype(BF16).astype(F32)
    n = N_CTX * BLOCK
    back, maps = chunk_maps(iota((HALF * BACK, n), 1), iota((HALF * BACK, n), 0)), unpacking()
    lane = iota((n, 128), 1)
    halves = ((cot_near_ref, span, near_ref), (cot_far_ref, 0, far_ref))
    for half, (cot_ref, at, ref) in enumerate(halves):
        mine = half_of(values, half)
        inner = jnp.zeros((n, 1), F32)
        for i, block in enumerate(unpack(maps, cot_ref[:, at : at + width], cot_ref[:, at + width : at + span])):
            inner = inner + jnp.sum(block * mine[:, i * quarter : (i + 1) * quarter], axis=1, keepdims=True)
        turned = to_rows(spread(lane, 0, inner).astype(BF16))
        inner = turned[0:1] + turned[1:2] + turned[2:3]
        for i in range(N_CTX):
            inner_ref[i, 8 * half : 8 * half + 8, :] = jnp.broadcast_to(inner, (8, n))
        mine = (half_of(score, half) * mine).astype(BF16)
        ref[:, :width] = dot(back[0], mine).astype(BF16)
        extra = dot(back[1][0], mine[:, :quarter])
        for i in range(1, 4):
            extra = extra + dot(back[1][i], mine[:, i * quarter : (i + 1) * quarter])
        ref[:, width:] = extra.astype(BF16)


def relay_kernel(near_ref, x_all_ref, out_ref):
    out_ref[...] = near_ref[:, near_ref.shape[1] - out_ref.shape[1] :]


def grad_kernel(inner_ref, full_ref, near_ref, far_ref, out_ref):
    hid = full_ref.shape[2] - 128
    small = jnp.concatenate([full_ref[i, :, hid:].astype(F32) for i in range(N_CTX)], axis=0)
    grad = jnp.zeros((1, near_ref.shape[1]), F32)
    for half, x_ref in enumerate((near_ref, far_ref)):
        turned = to_rows(half_of(small, half).astype(BF16))
        score = turned[0:1] + turned[1:2] + turned[2:3]
        inner = inner_ref[0, 8 * half : 8 * half + 8, :]
        for i in range(1, N_CTX):
            inner = inner + inner_ref[i, 8 * half : 8 * half + 8, :]
        slope = inner * (score * (1.0 - score))
        a, b, c = (v.astype(F32) for v in pieces(slope))
        line = iota(slope.shape, 0)
        slope = jnp.where(line == 0, a, jnp.where(line == 1, b, jnp.where(line == 2, c, 0.0)))
        grad = grad + jnp.sum(dot(slope.astype(BF16), x_ref[...]), axis=0, keepdims=True)
    copies = out_ref.shape[0]
    lines = []
    for j in range(8):
        lines.append(grad[:, j * 128 : (j + 1) * 128])
    block = jnp.concatenate(lines, axis=0).astype(out_ref.dtype)
    for k in range(copies):
        out_ref[k] = block


def merge_kernel(near_ref, far_ref, grads_ref, out_ref):
    span = near_ref.shape[1]
    out_ref[:, :span] = near_ref[...]
    out_ref[:, span : 2 * span] = far_ref[...]
    parts = grads_ref.shape[0] // 2
    for zh in range(2):
        total = grads_ref[zh].astype(F32)
        for k in range(1, parts):
            total = total + grads_ref[2 * k + zh].astype(F32)
        high = total.astype(BF16)
        low = (total - high.astype(F32)).astype(BF16)
        for at, v in ((2 * span + zh * 128, high), (2 * span + 256 + zh * 128, low)):
            out_ref[:, at : at + 128] = jnp.concatenate([v.astype(F32)] * HALF, axis=0).astype(BF16)


def out_kernel(zh_ref, routes_ref, fin_ref, out_ref, grad_ref):
    far, place, position = where_to(zh_ref[0], routes_ref[...])
    count, width = out_ref.shape
    quarter = width // 4
    span = width + quarter
    n = HALF * BACK
    slots = iota((count, n), 1)
    base = place * BACK
    for half in range(2):
        here = far == half
        of_main = pick((slots == base + position) & (position < BACK) & here)
        main = dot(of_main, fin_ref[:, half * span : half * span + width])
        extra = fin_ref[:, half * span + width : (half + 1) * span]
        for i in range(4):
            cols = slice(i * quarter, (i + 1) * quarter)
            of_extra = pick((slots == base + (position - BACK) * 4 + i) & (position >= BACK) & here)
            value = main[:, cols] + dot(of_extra, extra)
            if half:
                value = value + out_ref[:, cols].astype(F32)
            out_ref[:, cols] = value.astype(BF16)
    line, r = iota((N_EXP, n), 0), iota((N_EXP, n), 1)
    place = jnp.where(line >= HALF, line - HALF, line)
    for j in range(8):
        total = jnp.zeros((N_EXP, 128), F32)
        for zh in range(2):
            take = pick((r == place * BACK + j) & ((line >= HALF) == (zh == 1)))
            for part in range(2):
                at = 2 * span + part * 256 + zh * 128
                total = total + dot(take, fin_ref[:, at : at + 128])
        grad_ref[:, j * 128 : (j + 1) * 128] = total


def call(kernel, out, scalars=0, scratch=()):
    def run(*args):
        smem = pl.BlockSpec(memory_space=pltpu.SMEM)
        vmem = pl.BlockSpec(memory_space=pltpu.VMEM)
        specs = [smem if i < scalars else vmem for i in range(len(args))]
        return pl.pallas_call(
            kernel,
            in_specs=specs,
            out_specs=jax.tree.map(lambda _: vmem, out),
            out_shape=out,
            scratch_shapes=scratch,
            compiler_params=pltpu.CompilerParams(vmem_limit_bytes=16 * 1024 * 1024),
        )(*args)

    return run


def as_one_step(turns, body, state):
    out = lax.while_loop(lambda s: s[0] < turns, lambda s: (s[0] + 1, *body(s[0], *s[1:])), (jnp.int32(0), *state))
    return out[1:]


def shards(tokens, routes, router_weight, gate_weight, up_weight, down_weight, cotangent):
    count, width = tokens.shape
    routes = routes.reshape(1, count)
    hid = gate_weight.shape[2]
    shape = jax.ShapeDtypeStruct
    zh = lax.axis_index("zh").astype(I32)
    expert = zh * HALF + lax.axis_index("y") * 2 + lax.axis_index("core")
    zh = zh.reshape(1)
    turns = 1 + lax.axis_index("ctx").astype(I32) // N_CTX
    span = width + width // 4
    exchange = functools.partial(lax.all_to_all, axis_name=IN_Z, split_axis=0, concat_axis=0, tiled=True)
    over_ctx = functools.partial(lax.all_to_all, axis_name="ctx", split_axis=0, concat_axis=0, tiled=True)

    chunk = shape((HALF * BACK, span), BF16)
    wide = shape((N_CTX * BLOCK, width), BF16)
    part = shape((N_CTX, BLOCK, 2 * hid + 128), BF16)
    whole = shape((N_CTX, 2 * BLOCK, hid + 128), BF16)
    x_far, near, x, mine, full = call(
        pack_kernel,
        (chunk, shape((HALF * BACK, 3 * span), BF16), wide, part, whole),
        1,
    )(zh, routes, tokens, cotangent)
    router_col = lax.dynamic_slice(router_weight, (lax.axis_index("ctx") * width, expert), (width, 1))
    router_col = jnp.concatenate([*pieces(router_col), jnp.zeros((width, 125), BF16)], axis=1)
    weights = router_col, gate_weight[0], up_weight[0]
    x_far = lax.ppermute(x_far, PAIR, PAIR_PERM)

    def near_half(turn, near, x, mine):
        near = exchange(near)
        sums, x = call(up_kernel, (part, wide), 1)(turn.reshape(1), near, *weights)
        return near, x, over_ctx(sums)

    near, x_near, mine_near = as_one_step(turns, near_half, (near, x, mine))
    x_all = exchange(x_far)
    cot_far = lax.ppermute(call(relay_kernel, chunk)(near, x_all), PAIR, PAIR_PERM)

    def to_hidden(turn, x, full):
        sums, x = call(up_kernel, (part, wide), 1)(turn.reshape(1), x_all, *weights)
        return x, over_ctx(call(hidden_kernel, whole)(mine_near, over_ctx(sums)))

    x_far, full = as_one_step(turns, to_hidden, (x, full))

    near_back, far, inner = call(
        down_kernel,
        (chunk, chunk, shape((N_CTX, 16, N_CTX * BLOCK), F32)),
    )(full, near, cot_far, down_weight[0])
    far = lax.ppermute(far, PAIR, PAIR_PERM)
    inner = over_ctx(inner)
    grad = call(grad_kernel, shape((lax.axis_size(ALL_Z), 8, width // 8), BF16))(inner, full, x_near, x_far)

    (grads,) = as_one_step(turns, lambda turn, v: (lax.all_to_all(v, ALL_Z, 0, 0, tiled=True),), (grad,))
    fin = exchange(call(merge_kernel, shape((HALF * BACK, 2 * span + 512), BF16))(near_back, far, grads))
    block_out, grad = call(out_kernel, (shape((count, width), BF16), shape((N_EXP, width), F32)), 1)(zh, routes, fin)
    return block_out, grad.T


def solution(mesh):
    fine = Mesh(mesh.devices.reshape(MESH), NAMES)
    ep = ("zh", "y", "core")
    return jax.shard_map(
        shards,
        mesh=fine,
        in_specs=(
            P(TOK, "ctx"),
            P(TOK, None),
            P(),
            P(ep, "ctx", None),
            P(ep, "ctx", None),
            P(ep, None, "ctx"),
            P(TOK, "ctx"),
        ),
        out_specs=(P(TOK, "ctx"), P("ctx", None)),
        check_vma=False,
    )
```

```python
import functools

import jax
import jax.numpy as jnp
from jax import lax
from jax.experimental import pallas as pl
from jax.experimental.pallas import tpu as pltpu
from jax.sharding import Mesh, PartitionSpec as P

BF16 = jnp.bfloat16
F32 = jnp.float32
I32 = jnp.int32
CAP = 10
N_EXP = 16
N_CTX = 4
HALF = 8
BACK = 8
MESH = (2, 8, 4, 2, 4, 2)
NAMES = ("dh", "dl", "ctx", "zh", "y", "core")
TOK = ("dh", "dl", "zh", "y", "core")
ALL_Z = ("dh", "dl", "zh")
IN_Z = ("y", "core")
PAIR = ("dh", "zh")
PAIR_PERM = ((0, 3), (3, 0), (1, 2), (2, 1))


def dot(a, b, dims=((1,), (0,))):
    return lax.dot_general(a, b, (dims, ((), ())), preferred_element_type=F32)


def iota(shape, dim):
    return lax.broadcasted_iota(I32, shape, dim)


def pick(mask):
    return mask.astype(F32).astype(BF16)


def pieces(v):
    a = v.astype(BF16)
    v = v - a.astype(F32)
    b = v.astype(BF16)
    c = (v - b.astype(F32)).astype(BF16)
    return a, b, c


def spread(lane, first, v):
    a, b, c = pieces(v)
    out = jnp.where(lane == first, a.astype(F32), 0.0)
    out = jnp.where(lane == first + 1, b.astype(F32), out)
    return jnp.where(lane == first + 2, c.astype(F32), out)


def gathered(lane, first, v):
    return jnp.sum(jnp.where((lane >= first) & (lane < first + 3), v, 0.0), axis=1, keepdims=True)


def tenth(r):
    out = jnp.zeros_like(r)
    for k in range(1, HALF):
        out = out + (r >= k * CAP).astype(I32)
    return out


def where_to(zh, routes):
    count = routes.shape[1]
    own = iota((count, count), 0) == iota((count, count), 1)
    route = jnp.sum(jnp.where(own, routes, 0).astype(F32), axis=1, keepdims=True).astype(I32)
    ids = iota((count, 128), 1)
    onehot = (route == ids).astype(F32)
    before = pick(iota((count, count), 1) < iota((count, count), 0))
    earlier = dot(before, onehot.astype(BF16))
    position = jnp.sum(earlier * onehot, axis=1, keepdims=True).astype(I32)
    far = jnp.where(route >= HALF, 1, 0)
    far = jnp.where(zh == 1, 1 - far, far)
    place = jnp.where(route >= HALF, route - HALF, route)
    return far, place, position


def packing(base, position, shape):
    slots = iota(shape, 1)
    whole = pick((slots == base + position) & (position < BACK))
    quarters = [pick((slots == base + (position - BACK) * 4 + i) & (position >= BACK)) for i in range(4)]
    return whole, quarters


def pack_kernel(zh_ref, routes_ref, tok_ref, cot_ref, far_ref, near_ref, x_ref, full_ref):
    x_ref[...] = jnp.zeros(x_ref.shape, BF16)
    full_ref[...] = jnp.zeros(full_ref.shape, BF16)
    far, place, position = where_to(zh_ref[0], routes_ref[...])
    count, width = tok_ref.shape
    quarter = width // 4
    span = width + quarter
    n = HALF * BACK
    whole, quarters = packing(far * n + place * BACK, position, (count, 2 * n))
    turn = ((0,), (0,))
    for ref, near_at, far_out, far_at in ((tok_ref, 0, far_ref, 0), (cot_ref, span, near_ref, 2 * span)):
        main = dot(whole, ref[...], turn).astype(BF16)
        extra = dot(quarters[0], ref[:, :quarter], turn)
        for i in range(1, 4):
            extra = extra + dot(quarters[i], ref[:, i * quarter : (i + 1) * quarter], turn)
        extra = extra.astype(BF16)
        near_ref[:, near_at : near_at + width], near_ref[:, near_at + width : near_at + span] = main[:n], extra[:n]
        far_out[:, far_at : far_at + width], far_out[:, far_at + width : far_at + span] = main[n:], extra[n:]


def unpacking():
    shape = (HALF * CAP, HALF * BACK)
    r, col = iota(shape, 0), iota(shape, 1)
    src = tenth(r)
    p = r - src * CAP
    whole = pick((col == src * BACK + p) & (p < BACK))
    quarters = [pick((col == src * BACK + (p - BACK) * 4 + i) & (p >= BACK)) for i in range(4)]
    return whole, quarters


def unpack(maps, main, extra):
    whole, quarters = maps
    quarter = extra.shape[1]
    return [dot(whole, main[:, i * quarter : (i + 1) * quarter]) + dot(quarters[i], extra) for i in range(4)]


def up_kernel(turn_ref, near_ref, far_ref, router_ref, gate_ref, up_ref, part_ref, x_ref):
    width, hid = gate_ref.shape
    quarter = width // 4
    span = width + quarter
    n = HALF * CAP
    maps = unpacking()
    for half, ref in enumerate((near_ref, far_ref)):
        for i, block in enumerate(unpack(maps, ref[:, :width], ref[:, width:span])):
            x_ref[half * n : (half + 1) * n, i * quarter : (i + 1) * quarter] = block.astype(BF16)
    x = x_ref[...]
    rows = 2 * n // N_CTX

    def put(v, at):
        for i in range(N_CTX):
            part_ref[i, :, at : at + v.shape[1]] = v[i * rows : (i + 1) * rows].astype(BF16)

    logit = jnp.sum(dot(x, router_ref[...]), axis=1, keepdims=True)
    put(spread(iota((2 * n, 128), 1), 0, logit), 2 * hid)
    put(dot(x, gate_ref[...]), 0)
    put(dot(x, up_ref[...]), hid)


def hidden_kernel(mine_ref, out_ref):
    hid = (mine_ref.shape[2] - 128) // 2

    def total(at, size):
        out = mine_ref[0, :, at : at + size].astype(F32)
        for i in range(1, N_CTX):
            out = out + mine_ref[i, :, at : at + size].astype(F32)
        return out

    gate, up = total(0, hid), total(hid, hid)
    logit = jnp.sum(total(2 * hid, 128), axis=1, keepdims=True)
    hidden = (gate / (1.0 + jnp.exp(-gate)) * up).astype(BF16)
    score = 1.0 / (1.0 + jnp.exp(-logit))
    small = spread(iota((hidden.shape[0], 128), 1), 0, score).astype(BF16)
    for i in range(N_CTX):
        out_ref[i, :, :hid] = hidden
        out_ref[i, :, hid:] = small


def to_rows(v):
    size = v.shape[0]
    eye = pick(iota((size, size), 0) == iota((size, size), 1))
    return dot(v, eye, ((0,), (0,)))


def down_kernel(full_ref, cot_near_ref, cot_far_ref, down_ref, near_ref, far_ref, inner_ref, values_ref):
    hid, width = down_ref.shape
    quarter = width // 4
    span = width + quarter
    full = jnp.concatenate([full_ref[i].astype(F32) for i in range(N_CTX)], axis=0)
    rows = full.shape[0]
    lane = iota((rows, 128), 1)
    score = gathered(lane, 0, full[:, hid:])
    values_ref[...] = dot(full[:, :hid].astype(BF16), down_ref[...]).astype(BF16)
    n = HALF * CAP
    maps = unpacking()
    sums = []
    for half, (ref, at) in enumerate(((cot_near_ref, span), (cot_far_ref, 0))):
        inner = jnp.zeros((n, 1), F32)
        for i, block in enumerate(unpack(maps, ref[:, at : at + width], ref[:, at + width : at + span])):
            value = values_ref[half * n : (half + 1) * n, i * quarter : (i + 1) * quarter].astype(F32)
            inner = inner + jnp.sum(block * value, axis=1, keepdims=True)
        sums.append(inner)
    turned = to_rows(spread(lane, 0, jnp.concatenate(sums, axis=0)).astype(BF16))
    inner = turned[0:1] + turned[1:2] + turned[2:3]
    for i in range(N_CTX):
        inner_ref[i] = jnp.broadcast_to(inner, inner_ref.shape[1:])
    slot, r = iota((HALF * BACK, n), 0), iota((HALF * BACK, n), 1)
    src = tenth(r)
    p = r - src * CAP
    whole = pick((slot == src * BACK + p) & (p < BACK))
    quarters = [pick((slot == src * BACK + (p - BACK) * 4 + i) & (p >= BACK)) for i in range(4)]
    for half, ref in enumerate((near_ref, far_ref)):
        part = slice(half * n, (half + 1) * n)
        mine = (score[part] * values_ref[part, :].astype(F32)).astype(BF16)
        ref[:, :width] = dot(whole, mine).astype(BF16)
        extra = dot(quarters[0], mine[:, :quarter])
        for i in range(1, 4):
            extra = extra + dot(quarters[i], mine[:, i * quarter : (i + 1) * quarter])
        ref[:, width:] = extra.astype(BF16)


def slice_kernel(near_ref, out_ref):
    out_ref[...] = near_ref[:, near_ref.shape[1] - out_ref.shape[1] :]


def gate_kernel(v_ref, other_ref, out_ref):
    pass


def grad_kernel(inner_ref, full_ref, x_ref, out_ref):
    hid = full_ref.shape[2] - 128
    small = jnp.concatenate([full_ref[i, :, hid:].astype(F32) for i in range(N_CTX)], axis=0).astype(BF16)
    turned = to_rows(small)
    score = turned[0:1] + turned[1:2] + turned[2:3]
    inner = inner_ref[0]
    for i in range(1, N_CTX):
        inner = inner + inner_ref[i]
    slope = inner * (score * (1.0 - score))
    a, b, c = pieces(slope)
    line = iota(slope.shape, 0)
    slope = jnp.where(line == 0, a.astype(F32), jnp.where(line == 1, b.astype(F32), jnp.where(line == 2, c.astype(F32), 0.0)))
    grad = jnp.sum(dot(slope.astype(BF16), x_ref[...]), axis=0, keepdims=True)
    copies = out_ref.shape[0]
    lines = []
    for j in range(8):
        lines.append(grad[:, j * 128 : (j + 1) * 128])
    block = jnp.concatenate(lines, axis=0).astype(out_ref.dtype)
    for k in range(copies):
        out_ref[k] = block


def merge_kernel(near_ref, far_ref, grads_ref, out_ref):
    span = near_ref.shape[1]
    out_ref[:, :span] = near_ref[...]
    out_ref[:, span : 2 * span] = far_ref[...]
    parts = grads_ref.shape[0] // 2
    for zh in range(2):
        total = grads_ref[zh].astype(F32)
        for k in range(1, parts):
            total = total + grads_ref[2 * k + zh].astype(F32)
        high = total.astype(BF16)
        low = (total - high.astype(F32)).astype(BF16)
        for at, v in ((2 * span + zh * 128, high), (2 * span + 256 + zh * 128, low)):
            out_ref[:, at : at + 128] = jnp.concatenate([v.astype(F32)] * HALF, axis=0).astype(BF16)


def out_kernel(zh_ref, routes_ref, fin_ref, out_ref, grad_ref):
    far, place, position = where_to(zh_ref[0], routes_ref[...])
    count, width = out_ref.shape
    quarter = width // 4
    span = width + quarter
    n = HALF * BACK
    slots = iota((count, n), 1)
    base = place * BACK
    for half in range(2):
        here = far == half
        of_main = pick((slots == base + position) & (position < BACK) & here)
        main = dot(of_main, fin_ref[:, half * span : half * span + width])
        extra = fin_ref[:, half * span + width : (half + 1) * span]
        for i in range(4):
            cols = slice(i * quarter, (i + 1) * quarter)
            of_extra = pick((slots == base + (position - BACK) * 4 + i) & (position >= BACK) & here)
            value = main[:, cols] + dot(of_extra, extra)
            if half:
                value = value + out_ref[:, cols].astype(F32)
            out_ref[:, cols] = value.astype(BF16)
    line, r = iota((N_EXP, n), 0), iota((N_EXP, n), 1)
    place = jnp.where(line >= HALF, line - HALF, line)
    for j in range(8):
        total = jnp.zeros((N_EXP, 128), F32)
        for zh in range(2):
            take = pick((r == place * BACK + j) & ((line >= HALF) == (zh == 1)))
            for part in range(2):
                at = 2 * span + part * 256 + zh * 128
                total = total + dot(take, fin_ref[:, at : at + 128])
        grad_ref[:, j * 128 : (j + 1) * 128] = total


def call(kernel, out, scalars=0, scratch=(), aliases={}):
    def run(*args):
        smem = pl.BlockSpec(memory_space=pltpu.SMEM)
        vmem = pl.BlockSpec(memory_space=pltpu.VMEM)
        specs = [smem if i < scalars else vmem for i in range(len(args))]
        return pl.pallas_call(
            kernel,
            in_specs=specs,
            out_specs=jax.tree.map(lambda _: vmem, out),
            out_shape=out,
            scratch_shapes=scratch,
            input_output_aliases=aliases,
            compiler_params=pltpu.CompilerParams(vmem_limit_bytes=16 * 1024 * 1024),
        )(*args)

    return run


def as_one_step(turns, body, state):
    out = lax.while_loop(lambda s: s[0] < turns, lambda s: (s[0] + 1, *body(s[0], *s[1:])), (jnp.int32(0), *state))
    return out[1:]


def shards(tokens, routes, router_weight, gate_weight, up_weight, down_weight, cotangent):
    count, width = tokens.shape
    routes = routes.reshape(1, count)
    hid = gate_weight.shape[2]
    shape = jax.ShapeDtypeStruct
    zh = lax.axis_index("zh").astype(I32)
    expert = zh * HALF + lax.axis_index("y") * 2 + lax.axis_index("core")
    zh = zh.reshape(1)
    turns = 1 + lax.axis_index("ctx").astype(I32) // N_CTX
    span = width + width // 4
    rows = N_EXP * CAP
    exchange = functools.partial(lax.all_to_all, axis_name=IN_Z, split_axis=0, concat_axis=0, tiled=True)
    over_ctx = functools.partial(lax.all_to_all, axis_name="ctx", split_axis=0, concat_axis=0, tiled=True)

    chunk = shape((HALF * BACK, span), BF16)
    wide = shape((rows, width), BF16)
    x_far, near, x, full = call(
        pack_kernel,
        (chunk, shape((HALF * BACK, 3 * span), BF16), wide, shape((N_CTX, rows // N_CTX, hid + 128), BF16)),
        1,
    )(zh, routes, tokens, cotangent)
    x_far = lax.ppermute(x_far, PAIR, PAIR_PERM)
    (near,) = as_one_step(turns, lambda turn, v: (exchange(v),), (near,))
    x_all = exchange(x_far)
    cot_far = call(gate_kernel, chunk, aliases={0: 0})(call(slice_kernel, chunk)(near), x_all)
    cot_far = lax.ppermute(cot_far, PAIR, PAIR_PERM)

    router_col = lax.dynamic_slice(router_weight, (lax.axis_index("ctx") * width, expert), (width, 1))
    router_col = jnp.concatenate([*pieces(router_col), jnp.zeros((width, 125), BF16)], axis=1)
    part = shape((N_CTX, rows // N_CTX, 2 * hid + 128), BF16)

    def to_hidden(turn, x, full):
        weights = router_col, gate_weight[0], up_weight[0]
        sums, x = call(up_kernel, (part, wide), 1)(turn.reshape(1), near, x_all, *weights)
        return x, over_ctx(call(hidden_kernel, shape(full.shape, BF16))(over_ctx(sums)))

    x, full = as_one_step(turns, to_hidden, (x, full))

    near_back, far, inner = call(
        down_kernel,
        (chunk, chunk, shape((N_CTX, 8, rows), F32)),
        scratch=[pltpu.VMEM((rows, width), BF16)],
    )(full, near, cot_far, down_weight[0])
    far = lax.ppermute(far, PAIR, PAIR_PERM)
    inner = over_ctx(inner)
    grad = call(grad_kernel, shape((lax.axis_size(ALL_Z), 8, width // 8), BF16))(inner, full, x)

    (grads,) = as_one_step(turns, lambda turn, v: (lax.all_to_all(v, ALL_Z, 0, 0, tiled=True),), (grad,))
    fin = exchange(call(merge_kernel, shape((HALF * BACK, 2 * span + 512), BF16))(near_back, far, grads))
    block_out, grad = call(out_kernel, (shape((count, width), BF16), shape((N_EXP, width), F32)), 1)(zh, routes, fin)
    return block_out, grad.T


def solution(mesh):
    fine = Mesh(mesh.devices.reshape(MESH), NAMES)
    ep = ("zh", "y", "core")
    return jax.shard_map(
        shards,
        mesh=fine,
        in_specs=(
            P(TOK, "ctx"),
            P(TOK, None),
            P(),
            P(ep, "ctx", None),
            P(ep, "ctx", None),
            P(ep, None, "ctx"),
            P(TOK, "ctx"),
        ),
        out_specs=(P(TOK, "ctx"), P("ctx", None)),
        check_vma=False,
    )
```

```python
import functools

import jax
import jax.numpy as jnp
from jax import lax
from jax.experimental import pallas as pl
from jax.experimental.pallas import tpu as pltpu
from jax.sharding import Mesh, PartitionSpec as P

BF16 = jnp.bfloat16
F32 = jnp.float32
I32 = jnp.int32
CAP = 10
N_EXP = 16
N_CTX = 4
HALF = 8
BACK = 8
MESH = (2, 8, 4, 2, 4, 2)
NAMES = ("dh", "dl", "ctx", "zh", "y", "core")
TOK = ("dh", "dl", "zh", "y", "core")
ALL_Z = ("dh", "dl", "zh")
IN_Z = ("y", "core")
PAIR = ("dh", "zh")
PAIR_PERM = ((0, 3), (3, 0), (1, 2), (2, 1))


def dot(a, b, dims=((1,), (0,))):
    return lax.dot_general(a, b, (dims, ((), ())), preferred_element_type=F32)


def iota(shape, dim):
    return lax.broadcasted_iota(I32, shape, dim)


def pick(mask):
    return mask.astype(F32).astype(BF16)


def pieces(v):
    a = v.astype(BF16)
    v = v - a.astype(F32)
    b = v.astype(BF16)
    c = (v - b.astype(F32)).astype(BF16)
    return a, b, c


def spread(lane, first, v):
    a, b, c = pieces(v)
    out = jnp.where(lane == first, a.astype(F32), 0.0)
    out = jnp.where(lane == first + 1, b.astype(F32), out)
    return jnp.where(lane == first + 2, c.astype(F32), out)


def gathered(lane, first, v):
    return jnp.sum(jnp.where((lane >= first) & (lane < first + 3), v, 0.0), axis=1, keepdims=True)


def tenth(r):
    out = jnp.zeros_like(r)
    for k in range(1, HALF):
        out = out + (r >= k * CAP).astype(I32)
    return out


def where_to(zh, routes):
    count = routes.shape[1]
    own = iota((count, count), 0) == iota((count, count), 1)
    route = jnp.sum(jnp.where(own, routes, 0).astype(F32), axis=1, keepdims=True).astype(I32)
    ids = iota((count, 128), 1)
    onehot = (route == ids).astype(F32)
    before = pick(iota((count, count), 1) < iota((count, count), 0))
    earlier = dot(before, onehot.astype(BF16))
    position = jnp.sum(earlier * onehot, axis=1, keepdims=True).astype(I32)
    far = jnp.where(route >= HALF, 1, 0)
    far = jnp.where(zh == 1, 1 - far, far)
    place = jnp.where(route >= HALF, route - HALF, route)
    return far, place, position


def packing(base, position, shape):
    slots = iota(shape, 1)
    whole = pick((slots == base + position) & (position < BACK))
    quarters = [pick((slots == base + (position - BACK) * 4 + i) & (position >= BACK)) for i in range(4)]
    return whole, quarters


def pack_kernel(zh_ref, routes_ref, tok_ref, cot_ref, far_ref, near_ref, x_ref, full_ref):
    x_ref[...] = jnp.zeros(x_ref.shape, BF16)
    full_ref[...] = jnp.zeros(full_ref.shape, BF16)
    far, place, position = where_to(zh_ref[0], routes_ref[...])
    count, width = tok_ref.shape
    quarter = width // 4
    span = width + quarter
    n = HALF * BACK
    whole, quarters = packing(far * n + place * BACK, position, (count, 2 * n))
    turn = ((0,), (0,))
    for ref, near_at, far_out, far_at in ((tok_ref, 0, far_ref, 0), (cot_ref, span, near_ref, 2 * span)):
        main = dot(whole, ref[...], turn).astype(BF16)
        extra = dot(quarters[0], ref[:, :quarter], turn)
        for i in range(1, 4):
            extra = extra + dot(quarters[i], ref[:, i * quarter : (i + 1) * quarter], turn)
        extra = extra.astype(BF16)
        near_ref[:, near_at : near_at + width], near_ref[:, near_at + width : near_at + span] = main[:n], extra[:n]
        far_out[:, far_at : far_at + width], far_out[:, far_at + width : far_at + span] = main[n:], extra[n:]


def unpacking():
    shape = (HALF * CAP, HALF * BACK)
    r, col = iota(shape, 0), iota(shape, 1)
    src = tenth(r)
    p = r - src * CAP
    whole = pick((col == src * BACK + p) & (p < BACK))
    quarters = [pick((col == src * BACK + (p - BACK) * 4 + i) & (p >= BACK)) for i in range(4)]
    return whole, quarters


def unpack(maps, main, extra):
    whole, quarters = maps
    quarter = extra.shape[1]
    return [dot(whole, main[:, i * quarter : (i + 1) * quarter]) + dot(quarters[i], extra) for i in range(4)]


def up_kernel(turn_ref, near_ref, far_ref, router_ref, gate_ref, up_ref, part_ref, x_ref):
    width, hid = gate_ref.shape
    quarter = width // 4
    span = width + quarter
    n = HALF * CAP
    maps = unpacking()
    for half, ref in enumerate((near_ref, far_ref)):
        for i, block in enumerate(unpack(maps, ref[:, :width], ref[:, width:span])):
            x_ref[half * n : (half + 1) * n, i * quarter : (i + 1) * quarter] = block.astype(BF16)
    x = x_ref[...]
    rows = 2 * n // N_CTX

    def put(v, at):
        for i in range(N_CTX):
            part_ref[i, :, at : at + v.shape[1]] = v[i * rows : (i + 1) * rows].astype(BF16)

    logit = jnp.sum(dot(x, router_ref[...]), axis=1, keepdims=True)
    put(spread(iota((2 * n, 128), 1), 0, logit), 2 * hid)
    put(dot(x, gate_ref[...]), 0)
    put(dot(x, up_ref[...]), hid)


def hidden_kernel(mine_ref, out_ref):
    hid = (mine_ref.shape[2] - 128) // 2

    def total(at, size):
        out = mine_ref[0, :, at : at + size].astype(F32)
        for i in range(1, N_CTX):
            out = out + mine_ref[i, :, at : at + size].astype(F32)
        return out

    gate, up = total(0, hid), total(hid, hid)
    logit = jnp.sum(total(2 * hid, 128), axis=1, keepdims=True)
    hidden = (gate / (1.0 + jnp.exp(-gate)) * up).astype(BF16)
    score = 1.0 / (1.0 + jnp.exp(-logit))
    small = spread(iota((hidden.shape[0], 128), 1), 0, score).astype(BF16)
    for i in range(N_CTX):
        out_ref[i, :, :hid] = hidden
        out_ref[i, :, hid:] = small


def to_rows(v):
    size = v.shape[0]
    eye = pick(iota((size, size), 0) == iota((size, size), 1))
    return dot(v, eye, ((0,), (0,)))


def down_kernel(full_ref, cot_near_ref, cot_far_ref, down_ref, near_ref, far_ref, inner_ref, values_ref):
    hid, width = down_ref.shape
    quarter = width // 4
    span = width + quarter
    full = jnp.concatenate([full_ref[i].astype(F32) for i in range(N_CTX)], axis=0)
    rows = full.shape[0]
    lane = iota((rows, 128), 1)
    score = gathered(lane, 0, full[:, hid:])
    values_ref[...] = dot(full[:, :hid].astype(BF16), down_ref[...]).astype(BF16)
    n = HALF * CAP
    maps = unpacking()
    sums = []
    for half, (ref, at) in enumerate(((cot_near_ref, span), (cot_far_ref, 0))):
        inner = jnp.zeros((n, 1), F32)
        for i, block in enumerate(unpack(maps, ref[:, at : at + width], ref[:, at + width : at + span])):
            value = values_ref[half * n : (half + 1) * n, i * quarter : (i + 1) * quarter].astype(F32)
            inner = inner + jnp.sum(block * value, axis=1, keepdims=True)
        sums.append(inner)
    turned = to_rows(spread(lane, 0, jnp.concatenate(sums, axis=0)).astype(BF16))
    inner = turned[0:1] + turned[1:2] + turned[2:3]
    for i in range(N_CTX):
        inner_ref[i] = jnp.broadcast_to(inner, inner_ref.shape[1:])
    slot, r = iota((HALF * BACK, n), 0), iota((HALF * BACK, n), 1)
    src = tenth(r)
    p = r - src * CAP
    whole = pick((slot == src * BACK + p) & (p < BACK))
    quarters = [pick((slot == src * BACK + (p - BACK) * 4 + i) & (p >= BACK)) for i in range(4)]
    for half, ref in enumerate((near_ref, far_ref)):
        part = slice(half * n, (half + 1) * n)
        mine = (score[part] * values_ref[part, :].astype(F32)).astype(BF16)
        ref[:, :width] = dot(whole, mine).astype(BF16)
        extra = dot(quarters[0], mine[:, :quarter])
        for i in range(1, 4):
            extra = extra + dot(quarters[i], mine[:, i * quarter : (i + 1) * quarter])
        ref[:, width:] = extra.astype(BF16)


def slice_kernel(near_ref, out_ref):
    out_ref[...] = near_ref[:, near_ref.shape[1] - out_ref.shape[1] :]


def gate_kernel(v_ref, other_ref, out_ref):
    out_ref[...] = v_ref[...]


def grad_kernel(inner_ref, full_ref, x_ref, out_ref):
    hid = full_ref.shape[2] - 128
    small = jnp.concatenate([full_ref[i, :, hid:].astype(F32) for i in range(N_CTX)], axis=0).astype(BF16)
    turned = to_rows(small)
    score = turned[0:1] + turned[1:2] + turned[2:3]
    inner = inner_ref[0]
    for i in range(1, N_CTX):
        inner = inner + inner_ref[i]
    slope = inner * (score * (1.0 - score))
    a, b, c = pieces(slope)
    line = iota(slope.shape, 0)
    slope = jnp.where(line == 0, a.astype(F32), jnp.where(line == 1, b.astype(F32), jnp.where(line == 2, c.astype(F32), 0.0)))
    grad = jnp.sum(dot(slope.astype(BF16), x_ref[...]), axis=0, keepdims=True)
    copies = out_ref.shape[0]
    lines = []
    for j in range(8):
        lines.append(grad[:, j * 128 : (j + 1) * 128])
    block = jnp.concatenate(lines, axis=0).astype(out_ref.dtype)
    for k in range(copies):
        out_ref[k] = block


def merge_kernel(near_ref, far_ref, grads_ref, out_ref):
    span = near_ref.shape[1]
    out_ref[:, :span] = near_ref[...]
    out_ref[:, span : 2 * span] = far_ref[...]
    parts = grads_ref.shape[0] // 2
    for zh in range(2):
        total = grads_ref[zh].astype(F32)
        for k in range(1, parts):
            total = total + grads_ref[2 * k + zh].astype(F32)
        high = total.astype(BF16)
        low = (total - high.astype(F32)).astype(BF16)
        for at, v in ((2 * span + zh * 128, high), (2 * span + 256 + zh * 128, low)):
            out_ref[:, at : at + 128] = jnp.concatenate([v.astype(F32)] * HALF, axis=0).astype(BF16)


def out_kernel(zh_ref, routes_ref, fin_ref, out_ref, grad_ref):
    far, place, position = where_to(zh_ref[0], routes_ref[...])
    count, width = out_ref.shape
    quarter = width // 4
    span = width + quarter
    n = HALF * BACK
    slots = iota((count, n), 1)
    base = place * BACK
    for half in range(2):
        here = far == half
        of_main = pick((slots == base + position) & (position < BACK) & here)
        main = dot(of_main, fin_ref[:, half * span : half * span + width])
        extra = fin_ref[:, half * span + width : (half + 1) * span]
        for i in range(4):
            cols = slice(i * quarter, (i + 1) * quarter)
            of_extra = pick((slots == base + (position - BACK) * 4 + i) & (position >= BACK) & here)
            value = main[:, cols] + dot(of_extra, extra)
            if half:
                value = value + out_ref[:, cols].astype(F32)
            out_ref[:, cols] = value.astype(BF16)
    line, r = iota((N_EXP, n), 0), iota((N_EXP, n), 1)
    place = jnp.where(line >= HALF, line - HALF, line)
    for j in range(8):
        total = jnp.zeros((N_EXP, 128), F32)
        for zh in range(2):
            take = pick((r == place * BACK + j) & ((line >= HALF) == (zh == 1)))
            for part in range(2):
                at = 2 * span + part * 256 + zh * 128
                total = total + dot(take, fin_ref[:, at : at + 128])
        grad_ref[:, j * 128 : (j + 1) * 128] = total


def call(kernel, out, scalars=0, scratch=()):
    def run(*args):
        smem = pl.BlockSpec(memory_space=pltpu.SMEM)
        vmem = pl.BlockSpec(memory_space=pltpu.VMEM)
        specs = [smem if i < scalars else vmem for i in range(len(args))]
        return pl.pallas_call(
            kernel,
            in_specs=specs,
            out_specs=jax.tree.map(lambda _: vmem, out),
            out_shape=out,
            scratch_shapes=scratch,
            compiler_params=pltpu.CompilerParams(vmem_limit_bytes=16 * 1024 * 1024),
        )(*args)

    return run


def as_one_step(turns, body, state):
    out = lax.while_loop(lambda s: s[0] < turns, lambda s: (s[0] + 1, *body(s[0], *s[1:])), (jnp.int32(0), *state))
    return out[1:]


def shards(tokens, routes, router_weight, gate_weight, up_weight, down_weight, cotangent):
    count, width = tokens.shape
    routes = routes.reshape(1, count)
    hid = gate_weight.shape[2]
    shape = jax.ShapeDtypeStruct
    zh = lax.axis_index("zh").astype(I32)
    expert = zh * HALF + lax.axis_index("y") * 2 + lax.axis_index("core")
    zh = zh.reshape(1)
    turns = 1 + lax.axis_index("ctx").astype(I32) // N_CTX
    span = width + width // 4
    rows = N_EXP * CAP
    exchange = functools.partial(lax.all_to_all, axis_name=IN_Z, split_axis=0, concat_axis=0, tiled=True)
    over_ctx = functools.partial(lax.all_to_all, axis_name="ctx", split_axis=0, concat_axis=0, tiled=True)

    chunk = shape((HALF * BACK, span), BF16)
    wide = shape((rows, width), BF16)
    x_far, near, x, full = call(
        pack_kernel,
        (chunk, shape((HALF * BACK, 3 * span), BF16), wide, shape((N_CTX, rows // N_CTX, hid + 128), BF16)),
        1,
    )(zh, routes, tokens, cotangent)
    x_far = lax.ppermute(x_far, PAIR, PAIR_PERM)
    (near,) = as_one_step(turns, lambda turn, v: (exchange(v),), (near,))
    x_all = exchange(x_far)
    cot_far = call(gate_kernel, chunk)(call(slice_kernel, chunk)(near), x_all)
    cot_far = lax.ppermute(cot_far, PAIR, PAIR_PERM)

    router_col = lax.dynamic_slice(router_weight, (lax.axis_index("ctx") * width, expert), (width, 1))
    router_col = jnp.concatenate([*pieces(router_col), jnp.zeros((width, 125), BF16)], axis=1)
    part = shape((N_CTX, rows // N_CTX, 2 * hid + 128), BF16)

    def to_hidden(turn, x, full):
        weights = router_col, gate_weight[0], up_weight[0]
        sums, x = call(up_kernel, (part, wide), 1)(turn.reshape(1), near, x_all, *weights)
        return x, over_ctx(call(hidden_kernel, shape(full.shape, BF16))(over_ctx(sums)))

    x, full = as_one_step(turns, to_hidden, (x, full))

    near_back, far, inner = call(
        down_kernel,
        (chunk, chunk, shape((N_CTX, 8, rows), F32)),
        scratch=[pltpu.VMEM((rows, width), BF16)],
    )(full, near, cot_far, down_weight[0])
    far = lax.ppermute(far, PAIR, PAIR_PERM)
    inner = over_ctx(inner)
    grad = call(grad_kernel, shape((lax.axis_size(ALL_Z), 8, width // 8), BF16))(inner, full, x)

    (grads,) = as_one_step(turns, lambda turn, v: (lax.all_to_all(v, ALL_Z, 0, 0, tiled=True),), (grad,))
    fin = exchange(call(merge_kernel, shape((HALF * BACK, 2 * span + 512), BF16))(near_back, far, grads))
    block_out, grad = call(out_kernel, (shape((count, width), BF16), shape((N_EXP, width), F32)), 1)(zh, routes, fin)
    return block_out, grad.T


def solution(mesh):
    fine = Mesh(mesh.devices.reshape(MESH), NAMES)
    ep = ("zh", "y", "core")
    return jax.shard_map(
        shards,
        mesh=fine,
        in_specs=(
            P(TOK, "ctx"),
            P(TOK, None),
            P(),
            P(ep, "ctx", None),
            P(ep, "ctx", None),
            P(ep, None, "ctx"),
            P(TOK, "ctx"),
        ),
        out_specs=(P(TOK, "ctx"), P("ctx", None)),
        check_vma=False,
    )
```

```python
import functools

import jax
import jax.numpy as jnp
from jax import lax
from jax.experimental import pallas as pl
from jax.experimental.pallas import tpu as pltpu
from jax.sharding import Mesh, PartitionSpec as P

BF16 = jnp.bfloat16
F32 = jnp.float32
I32 = jnp.int32
CAP = 10
N_EXP = 16
N_CTX = 4
HALF = 8
BACK = 8
MESH = (2, 8, 4, 2, 4, 2)
NAMES = ("dh", "dl", "ctx", "zh", "y", "core")
TOK = ("dh", "dl", "zh", "y", "core")
ALL_Z = ("dh", "dl", "zh")
IN_Z = ("y", "core")
PAIR = ("dh", "zh")
PAIR_PERM = ((0, 3), (3, 0), (1, 2), (2, 1))


def dot(a, b, dims=((1,), (0,))):
    return lax.dot_general(a, b, (dims, ((), ())), preferred_element_type=F32)


def iota(shape, dim):
    return lax.broadcasted_iota(I32, shape, dim)


def pick(mask):
    return mask.astype(F32).astype(BF16)


def pieces(v):
    a = v.astype(BF16)
    v = v - a.astype(F32)
    b = v.astype(BF16)
    c = (v - b.astype(F32)).astype(BF16)
    return a, b, c


def spread(lane, first, v):
    a, b, c = pieces(v)
    out = jnp.where(lane == first, a.astype(F32), 0.0)
    out = jnp.where(lane == first + 1, b.astype(F32), out)
    return jnp.where(lane == first + 2, c.astype(F32), out)


def gathered(lane, first, v):
    return jnp.sum(jnp.where((lane >= first) & (lane < first + 3), v, 0.0), axis=1, keepdims=True)


def tenth(r):
    out = jnp.zeros_like(r)
    for k in range(1, HALF):
        out = out + (r >= k * CAP).astype(I32)
    return out


def where_to(zh, routes):
    count = routes.shape[1]
    own = iota((count, count), 0) == iota((count, count), 1)
    route = jnp.sum(jnp.where(own, routes, 0).astype(F32), axis=1, keepdims=True).astype(I32)
    ids = iota((count, 128), 1)
    onehot = (route == ids).astype(F32)
    before = pick(iota((count, count), 1) < iota((count, count), 0))
    earlier = dot(before, onehot.astype(BF16))
    position = jnp.sum(earlier * onehot, axis=1, keepdims=True).astype(I32)
    far = jnp.where(route >= HALF, 1, 0)
    far = jnp.where(zh == 1, 1 - far, far)
    place = jnp.where(route >= HALF, route - HALF, route)
    return far, place, position


def packing(base, position, shape):
    slots = iota(shape, 1)
    whole = pick((slots == base + position) & (position < BACK))
    quarters = [pick((slots == base + (position - BACK) * 4 + i) & (position >= BACK)) for i in range(4)]
    return whole, quarters


def pack_kernel(zh_ref, routes_ref, tok_ref, cot_ref, far_ref, near_ref, x_ref, full_ref):
    x_ref[...] = jnp.zeros(x_ref.shape, BF16)
    full_ref[...] = jnp.zeros(full_ref.shape, BF16)
    far, place, position = where_to(zh_ref[0], routes_ref[...])
    count, width = tok_ref.shape
    quarter = width // 4
    span = width + quarter
    n = HALF * BACK
    whole, quarters = packing(far * n + place * BACK, position, (count, 2 * n))
    turn = ((0,), (0,))
    for ref, near_at, far_out, far_at in ((tok_ref, 0, far_ref, 0), (cot_ref, span, near_ref, 2 * span)):
        main = dot(whole, ref[...], turn).astype(BF16)
        extra = dot(quarters[0], ref[:, :quarter], turn)
        for i in range(1, 4):
            extra = extra + dot(quarters[i], ref[:, i * quarter : (i + 1) * quarter], turn)
        extra = extra.astype(BF16)
        near_ref[:, near_at : near_at + width], near_ref[:, near_at + width : near_at + span] = main[:n], extra[:n]
        far_out[:, far_at : far_at + width], far_out[:, far_at + width : far_at + span] = main[n:], extra[n:]


def unpacking():
    shape = (HALF * CAP, HALF * BACK)
    r, col = iota(shape, 0), iota(shape, 1)
    src = tenth(r)
    p = r - src * CAP
    whole = pick((col == src * BACK + p) & (p < BACK))
    quarters = [pick((col == src * BACK + (p - BACK) * 4 + i) & (p >= BACK)) for i in range(4)]
    return whole, quarters


def unpack(maps, main, extra):
    whole, quarters = maps
    quarter = extra.shape[1]
    return [dot(whole, main[:, i * quarter : (i + 1) * quarter]) + dot(quarters[i], extra) for i in range(4)]


def up_kernel(turn_ref, near_ref, far_ref, router_ref, gate_ref, up_ref, part_ref, x_ref):
    width, hid = gate_ref.shape
    quarter = width // 4
    span = width + quarter
    n = HALF * CAP
    maps = unpacking()
    for half, ref in enumerate((near_ref, far_ref)):
        for i, block in enumerate(unpack(maps, ref[:, :width], ref[:, width:span])):
            x_ref[half * n : (half + 1) * n, i * quarter : (i + 1) * quarter] = block.astype(BF16)
    x = x_ref[...]
    rows = 2 * n // N_CTX

    def put(v, at):
        for i in range(N_CTX):
            part_ref[i, :, at : at + v.shape[1]] = v[i * rows : (i + 1) * rows].astype(BF16)

    logit = jnp.sum(dot(x, router_ref[...]), axis=1, keepdims=True)
    put(spread(iota((2 * n, 128), 1), 0, logit), 2 * hid)
    put(dot(x, gate_ref[...]), 0)
    put(dot(x, up_ref[...]), hid)


def hidden_kernel(mine_ref, out_ref):
    hid = (mine_ref.shape[2] - 128) // 2

    def total(at, size):
        out = mine_ref[0, :, at : at + size].astype(F32)
        for i in range(1, N_CTX):
            out = out + mine_ref[i, :, at : at + size].astype(F32)
        return out

    gate, up = total(0, hid), total(hid, hid)
    logit = jnp.sum(total(2 * hid, 128), axis=1, keepdims=True)
    hidden = (gate / (1.0 + jnp.exp(-gate)) * up).astype(BF16)
    score = 1.0 / (1.0 + jnp.exp(-logit))
    small = spread(iota((hidden.shape[0], 128), 1), 0, score).astype(BF16)
    for i in range(N_CTX):
        out_ref[i, :, :hid] = hidden
        out_ref[i, :, hid:] = small


def to_rows(v):
    size = v.shape[0]
    eye = pick(iota((size, size), 0) == iota((size, size), 1))
    return dot(v, eye, ((0,), (0,)))


def down_kernel(full_ref, cot_near_ref, cot_far_ref, down_ref, near_ref, far_ref, inner_ref, values_ref):
    hid, width = down_ref.shape
    quarter = width // 4
    span = width + quarter
    full = jnp.concatenate([full_ref[i].astype(F32) for i in range(N_CTX)], axis=0)
    rows = full.shape[0]
    lane = iota((rows, 128), 1)
    score = gathered(lane, 0, full[:, hid:])
    values_ref[...] = dot(full[:, :hid].astype(BF16), down_ref[...]).astype(BF16)
    n = HALF * CAP
    maps = unpacking()
    sums = []
    for half, (ref, at) in enumerate(((cot_near_ref, span), (cot_far_ref, 0))):
        inner = jnp.zeros((n, 1), F32)
        for i, block in enumerate(unpack(maps, ref[:, at : at + width], ref[:, at + width : at + span])):
            value = values_ref[half * n : (half + 1) * n, i * quarter : (i + 1) * quarter].astype(F32)
            inner = inner + jnp.sum(block * value, axis=1, keepdims=True)
        sums.append(inner)
    turned = to_rows(spread(lane, 0, jnp.concatenate(sums, axis=0)).astype(BF16))
    inner = turned[0:1] + turned[1:2] + turned[2:3]
    for i in range(N_CTX):
        inner_ref[i] = jnp.broadcast_to(inner, inner_ref.shape[1:])
    slot, r = iota((HALF * BACK, n), 0), iota((HALF * BACK, n), 1)
    src = tenth(r)
    p = r - src * CAP
    whole = pick((slot == src * BACK + p) & (p < BACK))
    quarters = [pick((slot == src * BACK + (p - BACK) * 4 + i) & (p >= BACK)) for i in range(4)]
    for half, ref in enumerate((near_ref, far_ref)):
        part = slice(half * n, (half + 1) * n)
        mine = (score[part] * values_ref[part, :].astype(F32)).astype(BF16)
        ref[:, :width] = dot(whole, mine).astype(BF16)
        extra = dot(quarters[0], mine[:, :quarter])
        for i in range(1, 4):
            extra = extra + dot(quarters[i], mine[:, i * quarter : (i + 1) * quarter])
        ref[:, width:] = extra.astype(BF16)


def slice_kernel(near_ref, out_ref):
    out_ref[...] = near_ref[:, near_ref.shape[1] - out_ref.shape[1] :]


def gate_kernel(v_ref, other_ref, out_ref):
    out_ref[...] = v_ref[...]


def grad_kernel(inner_ref, full_ref, x_ref, out_ref):
    hid = full_ref.shape[2] - 128
    small = jnp.concatenate([full_ref[i, :, hid:].astype(F32) for i in range(N_CTX)], axis=0).astype(BF16)
    turned = to_rows(small)
    score = turned[0:1] + turned[1:2] + turned[2:3]
    inner = inner_ref[0]
    for i in range(1, N_CTX):
        inner = inner + inner_ref[i]
    slope = inner * (score * (1.0 - score))
    a, b, c = pieces(slope)
    line = iota(slope.shape, 0)
    slope = jnp.where(line == 0, a.astype(F32), jnp.where(line == 1, b.astype(F32), jnp.where(line == 2, c.astype(F32), 0.0)))
    grad = jnp.sum(dot(slope.astype(BF16), x_ref[...]), axis=0, keepdims=True)
    copies = out_ref.shape[0]
    lines = []
    for j in range(8):
        lines.append(grad[:, j * 128 : (j + 1) * 128])
    block = jnp.concatenate(lines, axis=0).astype(out_ref.dtype)
    for k in range(copies):
        out_ref[k] = block


def merge_kernel(near_ref, far_ref, grads_ref, out_ref):
    span = near_ref.shape[1]
    out_ref[:, :span] = near_ref[...]
    out_ref[:, span : 2 * span] = far_ref[...]
    parts = grads_ref.shape[0] // 2
    for zh in range(2):
        total = grads_ref[zh].astype(F32)
        for k in range(1, parts):
            total = total + grads_ref[2 * k + zh].astype(F32)
        at = 2 * span + zh * 128
        out_ref[:, at : at + 128] = jnp.concatenate([total] * HALF, axis=0).astype(BF16)


def out_kernel(zh_ref, routes_ref, fin_ref, out_ref, grad_ref):
    far, place, position = where_to(zh_ref[0], routes_ref[...])
    count, width = out_ref.shape
    quarter = width // 4
    span = width + quarter
    n = HALF * BACK
    slots = iota((count, n), 1)
    base = place * BACK
    for half in range(2):
        here = far == half
        of_main = pick((slots == base + position) & (position < BACK) & here)
        main = dot(of_main, fin_ref[:, half * span : half * span + width])
        extra = fin_ref[:, half * span + width : (half + 1) * span]
        for i in range(4):
            cols = slice(i * quarter, (i + 1) * quarter)
            of_extra = pick((slots == base + (position - BACK) * 4 + i) & (position >= BACK) & here)
            value = main[:, cols] + dot(of_extra, extra)
            if half:
                value = value + out_ref[:, cols].astype(F32)
            out_ref[:, cols] = value.astype(BF16)
    line, r = iota((N_EXP, n), 0), iota((N_EXP, n), 1)
    place = jnp.where(line >= HALF, line - HALF, line)
    for j in range(8):
        total = jnp.zeros((N_EXP, 128), F32)
        for zh in range(2):
            take = pick((r == place * BACK + j) & ((line >= HALF) == (zh == 1)))
            at = 2 * span + zh * 128
            total = total + dot(take, fin_ref[:, at : at + 128])
        grad_ref[:, j * 128 : (j + 1) * 128] = total


def call(kernel, out, scalars=0, scratch=()):
    def run(*args):
        smem = pl.BlockSpec(memory_space=pltpu.SMEM)
        vmem = pl.BlockSpec(memory_space=pltpu.VMEM)
        specs = [smem if i < scalars else vmem for i in range(len(args))]
        return pl.pallas_call(
            kernel,
            in_specs=specs,
            out_specs=jax.tree.map(lambda _: vmem, out),
            out_shape=out,
            scratch_shapes=scratch,
            compiler_params=pltpu.CompilerParams(vmem_limit_bytes=16 * 1024 * 1024),
        )(*args)

    return run


def as_one_step(turns, body, state):
    out = lax.while_loop(lambda s: s[0] < turns, lambda s: (s[0] + 1, *body(s[0], *s[1:])), (jnp.int32(0), *state))
    return out[1:]


def shards(tokens, routes, router_weight, gate_weight, up_weight, down_weight, cotangent):
    count, width = tokens.shape
    routes = routes.reshape(1, count)
    hid = gate_weight.shape[2]
    shape = jax.ShapeDtypeStruct
    zh = lax.axis_index("zh").astype(I32)
    expert = zh * HALF + lax.axis_index("y") * 2 + lax.axis_index("core")
    zh = zh.reshape(1)
    turns = 1 + lax.axis_index("ctx").astype(I32) // N_CTX
    span = width + width // 4
    rows = N_EXP * CAP
    exchange = functools.partial(lax.all_to_all, axis_name=IN_Z, split_axis=0, concat_axis=0, tiled=True)
    over_ctx = functools.partial(lax.all_to_all, axis_name="ctx", split_axis=0, concat_axis=0, tiled=True)

    chunk = shape((HALF * BACK, span), BF16)
    wide = shape((rows, width), BF16)
    x_far, near, x, full = call(
        pack_kernel,
        (chunk, shape((HALF * BACK, 3 * span), BF16), wide, shape((N_CTX, rows // N_CTX, hid + 128), BF16)),
        1,
    )(zh, routes, tokens, cotangent)
    x_far = lax.ppermute(x_far, PAIR, PAIR_PERM)
    (near,) = as_one_step(turns, lambda turn, v: (exchange(v),), (near,))
    x_all = exchange(x_far)
    cot_far = call(gate_kernel, chunk)(call(slice_kernel, chunk)(near), x_all)
    cot_far = lax.ppermute(cot_far, PAIR, PAIR_PERM)

    router_col = lax.dynamic_slice(router_weight, (lax.axis_index("ctx") * width, expert), (width, 1))
    router_col = jnp.concatenate([*pieces(router_col), jnp.zeros((width, 125), BF16)], axis=1)
    part = shape((N_CTX, rows // N_CTX, 2 * hid + 128), BF16)

    def to_hidden(turn, x, full):
        weights = router_col, gate_weight[0], up_weight[0]
        sums, x = call(up_kernel, (part, wide), 1)(turn.reshape(1), near, x_all, *weights)
        return x, over_ctx(call(hidden_kernel, shape(full.shape, BF16))(over_ctx(sums)))

    x, full = as_one_step(turns, to_hidden, (x, full))

    near_back, far, inner = call(
        down_kernel,
        (chunk, chunk, shape((N_CTX, 8, rows), F32)),
        scratch=[pltpu.VMEM((rows, width), BF16)],
    )(full, near, cot_far, down_weight[0])
    far = lax.ppermute(far, PAIR, PAIR_PERM)
    inner = over_ctx(inner)
    grad = call(grad_kernel, shape((lax.axis_size(ALL_Z), 8, width // 8), BF16))(inner, full, x)

    (grads,) = as_one_step(turns, lambda turn, v: (lax.all_to_all(v, ALL_Z, 0, 0, tiled=True),), (grad,))
    fin = exchange(call(merge_kernel, shape((HALF * BACK, 2 * span + 256), BF16))(near_back, far, grads))
    block_out, grad = call(out_kernel, (shape((count, width), BF16), shape((N_EXP, width), F32)), 1)(zh, routes, fin)
    return block_out, grad.T


def solution(mesh):
    fine = Mesh(mesh.devices.reshape(MESH), NAMES)
    ep = ("zh", "y", "core")
    return jax.shard_map(
        shards,
        mesh=fine,
        in_specs=(
            P(TOK, "ctx"),
            P(TOK, None),
            P(),
            P(ep, "ctx", None),
            P(ep, "ctx", None),
            P(ep, None, "ctx"),
            P(TOK, "ctx"),
        ),
        out_specs=(P(TOK, "ctx"), P("ctx", None)),
        check_vma=False,
    )
```
